256 devices in a mesh: row: 8 (over z_hi, core), col: 32 (over z_lo, y, x).
Axes of the slice: x: 4, y: 4, z: 8 (z_hi: 4, z_lo: 2; z = z_hi * 2 + z_lo), core: 2. Of those that a mesh axis runs over, the one named last changes fastest.
Arguments:
- local_copy: float32 [2, 5120, 12288], P(None, 'row', 'col'), may hold values from -5 to 5
- dual: float32 [2, 5120, 12288], P(None, 'row', 'col'), may hold values from -4 to 4
- consensus: float32 [2, 4096, 8192], P(None, 'row', 'col'), may hold values from -5 to 5
- probe: float32 [2, 128, 128], replicated, may hold values from -6 to 6
- intensity: float32 [8192, 128, 128], P(('row', 'col')), may hold values from 0.1 to 24, as said below
- pos_rows: int32 [8192], P(('row', 'col')), may hold values from 0 to 4095, as said below
- pos_cols: int32 [8192], P(('row', 'col')), may hold values from 0 to 8191, as said below
Outputs:
- new_copy: float32 [2, 5120, 12288], P(None, 'row', 'col')
- new_consensus: float32 [2, 4096, 8192], P(None, 'row', 'col')
- new_dual: float32 [2, 5120, 12288], P(None, 'row', 'col')
- new_probe: float32 [2, 128, 128], replicated
The draws below stay inside these ranges and needn't reach their ends.
Inputs may be any that keep to these rules, and one draw needn't show every extreme that they name: `pos_rows`: pattern j starts in the rows of tile j // 32, tiles numbered a * 32 + b; in every tile one pattern starts on the tile's last row. `pos_cols`: pattern j starts in the columns of tile j // 32; in every tile one pattern starts on the tile's last column. `intensity`: Positive.
All inputs are finite; a program needn't handle non-finite values.
Results may differ from the reference program's by a relative error of at most 0.000065.
Values sent between devices are 32-bit elements; how exact they have to be, the bound alone decides.
A program may use at most 64 MiB of HBM per device.

```python
import jax
import jax.numpy as jnp
from jax import lax

PATCH = 128
TILE_R = 512
TILE_C = 256
PATCH_DEV = 32
EXT_R = 640
EXT_C = 384
NR = 4096
NC = 8192
PATCHES = 8192
N_ROW = 8
N_COL = 32


def draw_intensity(key, part):
    key = jax.random.fold_in(key, 11)
    place = jnp.arange(PATCHES, dtype=jnp.float32) / max(PATCHES - 1, 1)
    base_level = jnp.exp(jax.random.uniform(key, (PATCHES, PATCH, PATCH), jnp.float32, -1.5, 1.5))
    rising = 1.0 + 2.0 * place
    return base_level * rising[:, None, None]


def draw_pos_rows(key, part):
    key = jax.random.fold_in(key, 23)
    indices = jnp.arange(PATCHES, dtype=jnp.int32)
    owner = indices // PATCH_DEV
    offset = jax.random.randint(key, (PATCHES,), 0, TILE_R, dtype=jnp.int32)
    offset = jnp.where(indices % PATCH_DEV == 0, TILE_R - 1, offset)
    return owner // N_COL * TILE_R + offset


def draw_pos_cols(key, part):
    key = jax.random.fold_in(key, 37)
    indices = jnp.arange(PATCHES, dtype=jnp.int32)
    owner = indices // PATCH_DEV
    offset = jax.random.randint(key, (PATCHES,), 0, TILE_C, dtype=jnp.int32)
    offset = jnp.where(indices % PATCH_DEV == 1, TILE_C - 1, offset)
    return owner % N_COL * TILE_C + offset


def block_levels(stream_key, extent, shards, smallest, largest):
    factor_of, own = 1.0, jax.random.fold_in(stream_key, 6)
    for position, shards_of in shards:
        heights = jnp.exp(jax.random.uniform(jax.random.fold_in(own, position), (shards_of,), jnp.float32, smallest / len(shards), largest / len(shards)))
        factor_of = factor_of * jnp.repeat(heights, extent[position] // shards_of).reshape([-1 if axis == position else 1 for axis in range(len(extent))])
    return factor_of


def noise(own_key, shape, scale, limit, pieces=(), kind=jnp.bfloat16):
    entries = scale * jax.random.normal(own_key, shape, jnp.float32)
    if pieces:
        entries = entries * block_levels(own_key, shape, pieces, -0.22, 0.18)
    return jnp.clip(entries, -limit, limit).astype(kind)


def setup_inputs(seed: int = 0) -> dict:
    key_of = jax.random.split(jax.random.key(seed), 8)
    return {
        "local_copy": noise(key_of[0], (2, EXT_R * N_ROW, EXT_C * N_COL), 0.7, 5.0, ((1, 8), (2, 32)), jnp.float32),
        "dual": noise(key_of[1], (2, EXT_R * N_ROW, EXT_C * N_COL), 0.3, 4.0, ((1, 8), (2, 32)), jnp.float32),
        "consensus": noise(key_of[2], (2, NR, NC), 0.7, 5.0, ((1, 8), (2, 32)), jnp.float32),
        "probe": noise(key_of[3], (2, PATCH, PATCH), 1.0, 6.0, (), jnp.float32),
        "intensity": draw_intensity(jax.random.fold_in(key_of[7], 71), 0),
        "pos_rows": draw_pos_rows(jax.random.fold_in(key_of[7], 71), 0),
        "pos_cols": draw_pos_cols(jax.random.fold_in(key_of[7], 71), 0),
    }


object_step = 0.3
penalty = 1.0
probe_step = 0.5
epsilon = 1e-06

def device_gradient(copy_block, probe_field, patterns, top_rows, left_cols):
    field = copy_block[0] + 1j * copy_block[1]

    def take_window(top_row, left_col):
        return lax.dynamic_slice(field, (top_row, left_col), (PATCH, PATCH))
    patches = jax.vmap(take_window)(top_rows, left_cols)
    wave = probe_field[None] * patches
    spectrum = jnp.fft.fft2(wave, norm='ortho')
    power = spectrum.real ** 2 + spectrum.imag ** 2
    misfit = jnp.fft.ifft2((power - patterns) * spectrum, norm='ortho')
    object_grad = jnp.conj(probe_field)[None] * misfit
    probe_term = lax.optimization_barrier(jnp.sum(jnp.conj(patches) * misfit, axis=0))

    def add_patch(member, gradient):
        patch_term = jnp.stack([object_grad[member].real, object_grad[member].imag])
        top_row = top_rows[member]
        left_col = left_cols[member]
        zero_index = top_row * 0
        current = lax.dynamic_slice(gradient, (zero_index, top_row, left_col), (2, PATCH, PATCH))
        return lax.dynamic_update_slice(gradient, current + patch_term, (zero_index, top_row, left_col))
    gradient = lax.fori_loop(0, PATCH_DEV, add_patch, jnp.zeros((2, EXT_R, EXT_C), jnp.float32))
    return (gradient, jnp.stack([probe_term.real, probe_term.imag]), jnp.sum(gradient * gradient))

def reference(local_copy, dual, consensus, probe, intensity, pos_rows, pos_cols):
    devices = N_ROW * N_COL

    def to_blocks(field):
        shaped = field.reshape(2, N_ROW, EXT_R, N_COL, EXT_C).transpose(1, 3, 0, 2, 4)
        return shaped.reshape(devices, 2, EXT_R, EXT_C)

    def from_blocks(blocks):
        shaped = blocks.reshape(N_ROW, N_COL, 2, EXT_R, EXT_C).transpose(2, 0, 3, 1, 4)
        return shaped.reshape(2, N_ROW * EXT_R, N_COL * EXT_C)
    copies = to_blocks(local_copy)
    duals = to_blocks(dual)
    tile_row = jnp.arange(devices, dtype=jnp.int32) // N_COL
    tile_col = jnp.arange(devices, dtype=jnp.int32) % N_COL
    top_rows = pos_rows.reshape(devices, PATCH_DEV) - (tile_row * TILE_R)[:, None]
    left_cols = pos_cols.reshape(devices, PATCH_DEV) - (tile_col * TILE_C)[:, None]
    patterns = intensity.reshape(devices, PATCH_DEV, PATCH, PATCH)
    probe_field = probe[0] + 1j * probe[1]

    def one_device(inputs):
        return device_gradient(inputs[0], probe_field, inputs[1], inputs[2], inputs[3])
    gradients, probe_terms, norms = lax.map(one_device, (copies, patterns, top_rows, left_cols))
    probe_total = lax.optimization_barrier(jnp.sum(probe_terms, axis=0))
    norm_total = jnp.sum(norms)
    probe_rms = jnp.sqrt(jnp.sum(probe_total * probe_total) / (PATCH * PATCH) + epsilon)
    new_probe = probe - probe_step * probe_total / probe_rms
    grad_scale = 1.0 / jnp.sqrt(norm_total / (devices * EXT_R * EXT_C) + epsilon)

    def windows(field):
        padded = jnp.pad(field, ((0, 0), (0, PATCH), (0, PATCH)))

        def take_block(row_index, col_index):
            top = row_index * TILE_R
            return lax.dynamic_slice(padded, (top * 0, top, col_index * TILE_C), (2, EXT_R, EXT_C))
        return jax.vmap(take_block)(tile_row, tile_col)
    new_copies = copies - object_step * (grad_scale * gradients + penalty * (copies - windows(consensus) + duals))
    merged = new_copies + duals

    def add_block(device, state):
        total, cover = state
        top = tile_row[device] * TILE_R
        left = tile_col[device] * TILE_C
        zero_index = top * 0
        current = lax.dynamic_slice(total, (zero_index, top, left), (2, EXT_R, EXT_C))
        total = lax.dynamic_update_slice(total, current + merged[device], (zero_index, top, left))
        covered = lax.dynamic_slice(cover, (top, left), (EXT_R, EXT_C))
        cover = lax.dynamic_update_slice(cover, covered + 1.0, (top, left))
        return (total, cover)
    start_total = jnp.zeros((2, NR + PATCH, NC + PATCH), jnp.float32)
    start_cover = jnp.zeros((NR + PATCH, NC + PATCH), jnp.float32)
    total, cover = lax.fori_loop(0, devices, add_block, (start_total, start_cover))
    new_consensus = total[:, :NR, :NC] / cover[None, :NR, :NC]
    new_duals = duals + new_copies - windows(new_consensus)
    return (from_blocks(new_copies), new_consensus, from_blocks(new_duals), new_probe)
```

```python
import functools
import math

import jax
import jax.numpy as jnp
import ml_dtypes
import numpy as np
from jax import lax
from jax.experimental import pallas as pl
from jax.experimental.pallas import tpu as pltpu
from jax.sharding import PartitionSpec as P

MESH = pl.DeviceIdType.MESH
F32 = jnp.float32
BF16 = jnp.bfloat16
SIDE = 128
BATCH = 8
FAST = 8

object_step = 0.3
penalty = 1.0
probe_step = 0.5
epsilon = 1e-06


def dft_tables():
    index = np.arange(SIDE)
    angle = 2.0 * np.pi * ((index[:, None] * index[None, :]) % SIDE) / SIDE
    cosine = np.cos(angle) / math.sqrt(SIDE)
    sine = np.sin(angle) / math.sqrt(SIDE)
    forward = np.block([[cosine, -sine], [sine, cosine]])
    backward = np.block([[cosine, sine], [-sine, cosine]])
    parts = []
    for table in (forward, backward):
        high = table.astype(ml_dtypes.bfloat16)
        parts += [high, (table - high.astype(np.float64)).astype(ml_dtypes.bfloat16)]
    return np.stack(parts)


def halves(value):
    high = value.astype(BF16)
    return high, (value - high.astype(F32)).astype(BF16)


def times_right(value, high_table, low_table):
    high, low = halves(value)
    return jnp.dot(
        jnp.concatenate([high, low, high], 1),
        jnp.concatenate([high_table, high_table, low_table], 0),
        preferred_element_type=F32,
    )


def times_left(high_table, low_table, value):
    high, low = halves(value)
    return jnp.dot(
        jnp.concatenate([high_table, low_table, high_table], 1),
        jnp.concatenate([high, high, low], 0),
        preferred_element_type=F32,
    )


def swapped(value):
    s = SIDE
    return jnp.concatenate(
        [
            jnp.concatenate([value[:s, :s], value[s:, :s]], 1),
            jnp.concatenate([value[:s, s:], value[s:, s:]], 1),
        ],
        0,
    )


def patch_body(
    rows_ref, cols_ref, copy_hbm, probe_ref, data_hbm, tables_ref,
    grad_ref, probe_grad_ref, norm_ref,
    copy_ref, data_ref, sems,
):
    s = SIDE
    count = data_ref.shape[0]
    blocks, ext_rows = copy_ref.shape[1:3]
    tile_rows, tile_cols = ext_rows - s, (blocks - 1) * s
    moves = []
    for block in range(blocks):
        moves.append(
            pltpu.make_async_copy(
                copy_hbm.at[:, :, pl.ds(block * s, s)], copy_ref.at[:, block], sems.at[block]
            )
        )
    for part in range(count // BATCH):
        span = pl.ds(part * BATCH, BATCH)
        moves.append(
            pltpu.make_async_copy(data_hbm.at[span], data_ref.at[span], sems.at[blocks + part])
        )
    for move in moves:
        move.start()
    grad_ref[...] = jnp.zeros_like(grad_ref)
    probe_grad_ref[...] = jnp.zeros_like(probe_grad_ref)
    lane = lax.broadcasted_iota(jnp.int32, (s, s), 1)
    for move in moves:
        move.wait()

    def step(index, carry):
        forward = (tables_ref[0], tables_ref[1])
        backward = (tables_ref[2], tables_ref[3])
        probe_re, probe_im = probe_ref[0], probe_ref[1]
        places, fields = [], []
        for member in range(BATCH):
            top = rows_ref[index * BATCH + member] & (tile_rows - 1)
            left = cols_ref[index * BATCH + member] & (tile_cols - 1)
            block, shift = left // s, left % s
            places.append((top, block, shift))
            field = []
            for part in range(2):
                near = copy_ref[part, block, pl.ds(top, s), :]
                far = copy_ref[part, block + 1, pl.ds(top, s), :]
                field.append(pltpu.roll(jnp.where(lane >= shift, near, far), (s - shift) % s, 1))
            fields.append(field)
        sum_re = jnp.zeros((s, s), F32)
        sum_im = jnp.zeros((s, s), F32)
        for first in range(0, BATCH, 2):
            wave = jnp.concatenate(
                [
                    jnp.concatenate(
                        [probe_re * re - probe_im * im, probe_re * im + probe_im * re], 1
                    )
                    for re, im in fields[first : first + 2]
                ],
                0,
            )
            spectrum = times_left(*backward, swapped(times_right(wave, *forward)))
            spec_re, spec_im = spectrum[:s], spectrum[s:]
            data = jnp.concatenate(
                [data_ref[index * BATCH + first], data_ref[index * BATCH + first + 1]], 1
            )
            residue = spec_re * spec_re + spec_im * spec_im - data
            weighted = jnp.concatenate([residue * spec_re, residue * spec_im], 0)
            misfit = times_right(swapped(times_left(*forward, weighted)), *backward)
            for second in range(2):
                member = first + second
                mis_re = misfit[second * s : (second + 1) * s, :s]
                mis_im = misfit[second * s : (second + 1) * s, s:]
                re, im = fields[member]
                sum_re += re * mis_re + im * mis_im
                sum_im += re * mis_im - im * mis_re
                top, block, shift = places[member]
                terms = (probe_re * mis_re + probe_im * mis_im, probe_re * mis_im - probe_im * mis_re)
                for part in range(2):
                    term = pltpu.roll(terms[part], shift, 1)
                    grad_ref[part, block, pl.ds(top, s), :] += jnp.where(lane >= shift, term, 0.0)
                    grad_ref[part, block + 1, pl.ds(top, s), :] += jnp.where(lane >= shift, 0.0, term)
        probe_grad_ref[0] += sum_re
        probe_grad_ref[1] += sum_im
        return carry

    lax.fori_loop(0, count // BATCH, step, 0)

    def squares(index, total):
        for part in range(2):
            for block in range(blocks):
                value = grad_ref[part, block, pl.ds(pl.multiple_of(index * 8, 8), 8), :]
                total = total + value * value
        return total

    norm_ref[...] = lax.fori_loop(0, ext_rows // 8, squares, jnp.zeros((8, s), F32))


def patch_gradients(pos_rows, pos_cols, local_copy, probe, intensity):
    s = SIDE
    count = intensity.shape[0]
    ext_rows, ext_cols = local_copy.shape[1:]
    blocks = ext_cols // s
    vmem, smem = pl.BlockSpec(memory_space=pltpu.VMEM), pl.BlockSpec(memory_space=pltpu.SMEM)
    hbm = pl.BlockSpec(memory_space=pl.ANY)
    return pl.pallas_call(
        patch_body,
        in_specs=[smem, smem, hbm, vmem, hbm, vmem],
        out_specs=[vmem, vmem, vmem],
        out_shape=[
            jax.ShapeDtypeStruct((2, blocks, ext_rows, s), F32),
            jax.ShapeDtypeStruct((2, s, s), F32),
            jax.ShapeDtypeStruct((8, s), F32),
        ],
        scratch_shapes=[
            pltpu.VMEM((2, blocks, ext_rows, s), F32),
            pltpu.VMEM((count, s, s), F32),
            pltpu.SemaphoreType.DMA((blocks + count // BATCH,)),
        ],
        compiler_params=pltpu.CompilerParams(vmem_limit_bytes=50 * 2**20),
        cost_estimate=pl.CostEstimate(
            flops=count * 4 * 3 * 2 * s * 256 * 256, bytes_accessed=8 * 2**20, transcendentals=0
        ),
    )(pos_rows, pos_cols, local_copy, probe, intensity, jnp.asarray(dft_tables()))


def finish_body(
    n_row, n_col, fast, slow,
    copy_hbm, dual_hbm, grad_hbm, cons_hbm, up_hbm, left_hbm, diag_hbm, probe_grad_ref, norm_ref, probe_ref,
    new_copy_hbm, new_cons_hbm, new_dual_hbm, new_probe_ref,
    copy_v, dual_v, grad_v, cons_v, w_v, new_copy_v, new_cons_v, new_dual_v,
    from_up, from_down, from_left, from_right,
    fast_out, fast_in, slow_out, slow_in, row_out, row_in, slow_all, fast_all,
    load_sems, store_sems, halo_send, halo_recv, sum_send, sum_recv,
):
    s = SIDE
    a, b = lax.axis_index("row"), lax.axis_index("col")
    low, high = b % fast, b // fast
    ext_rows, ext_cols = copy_v.shape[1:]
    tile_rows, tile_cols = cons_v.shape[1] - s, cons_v.shape[2] - s
    blocks = ext_cols // s
    last = blocks - 1

    loads = []
    for index, (source, target) in enumerate(
        [
            (copy_hbm, copy_v),
            (dual_hbm, dual_v),
            (grad_hbm, grad_v),
            (cons_hbm, cons_v.at[:, pl.ds(0, tile_rows), pl.ds(0, tile_cols)]),
            (up_hbm, cons_v.at[:, pl.ds(tile_rows, s), pl.ds(0, tile_cols)]),
            (left_hbm, cons_v.at[:, pl.ds(0, tile_rows), pl.ds(tile_cols, s)]),
            (diag_hbm, cons_v.at[:, pl.ds(tile_rows, s), pl.ds(tile_cols, s)]),
        ]
    ):
        loads.append(pltpu.make_async_copy(source, target, load_sems.at[index]))
        loads[-1].start()

    up, down = ((a + n_row - 1) % n_row, b), ((a + 1) % n_row, b)
    left, right = (a, (b + n_col - 1) % n_col), (a, (b + 1) % n_col)

    def fast_peer(index):
        return (a, high * fast + index)

    def slow_peer(index):
        return (a, index * fast + low)

    def row_peer(index):
        return (index, b)

    groups = ((fast_peer, low, fast), (slow_peer, high, slow), (row_peer, a, n_row))
    greeted = [up, down, left, right]
    for peer, mine, size in groups:
        greeted += [peer((mine + hop) % size) for hop in range(1, size)]
    barrier = pltpu.get_barrier_semaphore()
    for device in greeted:
        pl.semaphore_signal(barrier, inc=1, device_id=device, device_id_type=MESH)
    pl.semaphore_wait(barrier, len(greeted))

    sent = []

    def send(source, target, send_sem, recv_sem, device):
        move = pltpu.make_async_remote_copy(
            src_ref=source, dst_ref=target, send_sem=send_sem, recv_sem=recv_sem,
            device_id=device, device_id_type=MESH,
        )
        move.start()
        sent.append(move)

    def spread(phase, group, source_of, slots):
        peer, mine, size = group
        for hop in range(1, size):
            other = (mine + hop) % size
            send(source_of(other), slots.at[mine], sum_send.at[phase, hop], sum_recv.at[phase, hop], peer(other))

        def arrived():
            for hop in range(1, size):
                other = (mine + size - hop) % size
                pltpu.make_async_remote_copy(
                    src_ref=source_of(other), dst_ref=slots.at[other], send_sem=sum_send.at[phase, hop],
                    recv_sem=sum_recv.at[phase, hop], device_id=peer(other), device_id_type=MESH,
                ).wait_recv()

        return arrived

    def total_of(slots, size):
        total = slots[0]
        for index in range(1, size):
            total = total + slots[index]
        return total

    share, piece = fast_out.shape[1] - 8, slow_out.shape[1] - 8
    for index in range(fast):
        fast_out[index, :share] = probe_grad_ref[pl.ds(index * share, share), :]
        fast_out[index, share:] = norm_ref[...]
    arrived = spread(0, groups[0], lambda other: fast_out.at[other], fast_in)
    fast_in[low] = fast_out[low]
    arrived()
    partial = total_of(fast_in, fast)
    for index in range(slow):
        slow_out[index, :piece] = partial[index * piece : (index + 1) * piece]
        slow_out[index, piece:] = partial[share:]
    arrived = spread(1, groups[1], lambda other: slow_out.at[other], slow_in)
    slow_in[high] = slow_out[high]
    arrived()
    row_out[...] = total_of(slow_in, slow)
    arrived = spread(2, groups[2], lambda other: row_out, row_in)
    row_in[a] = row_out[...]
    arrived()
    whole = total_of(row_in, n_row)
    slow_all[high] = whole[:piece]
    slow_arrived = spread(3, groups[1], lambda other: slow_all.at[high], slow_all)

    squares = jnp.sum(whole[piece:], keepdims=True)
    scale = object_step / jnp.sqrt(squares / (n_row * n_col * ext_rows * ext_cols) + epsilon)
    for load in loads:
        load.wait()

    keep = 1.0 - object_step * penalty

    def fill(first, count, block):
        columns = pl.ds(block * s, s)
        span = pl.ds(first, count)
        for part in range(2):
            old, dual = copy_v[part, span, columns], dual_v[part, span, columns]
            w_v[part, block, span, :] = keep * (old + dual) - scale * grad_v[part, block, span, :]

    for block in range(blocks):
        fill(0, s, block)
        fill(tile_rows, s, block)
    lower, upper, middle = pl.ds(tile_rows, s), pl.ds(0, s), pl.ds(s, tile_rows - s)
    send(w_v.at[:, :, upper], from_down, halo_send.at[0], halo_recv.at[0], up)
    send(w_v.at[:, :, lower], from_up, halo_send.at[1], halo_recv.at[1], down)
    fill(s, tile_rows - s, 0)
    fill(s, tile_rows - s, last)
    send(w_v.at[:, 0, middle], from_right.at[:, middle], halo_send.at[2], halo_recv.at[2], left)
    send(w_v.at[:, last, middle], from_left.at[:, middle], halo_send.at[3], halo_recv.at[3], right)
    for block in range(1, last):
        fill(s, tile_rows - s, block)

    def received(index):
        sent[first_halo + index].wait_recv()

    first_halo = len(sent) - 4

    slow_arrived()
    fast_all[low] = jnp.concatenate([slow_all[index] for index in range(slow)], 0)
    fast_arrived = spread(4, groups[0], lambda other: fast_all.at[low], fast_all)

    has_up, has_down = (a > 0).astype(F32), (a < n_row - 1).astype(F32)
    has_left, has_right = (b > 0).astype(F32), (b < n_col - 1).astype(F32)

    received(0)
    received(1)
    for part in range(2):
        for block in range(blocks):
            from_up[part, block] = w_v[part, block, upper] + has_up * from_up[part, block]
            from_down[part, block] = w_v[part, block, lower] + has_down * from_down[part, block]
    corner = len(sent)
    send(from_up.at[:, 0], from_right.at[:, upper], halo_send.at[4], halo_recv.at[4], left)
    send(from_down.at[:, 0], from_right.at[:, lower], halo_send.at[5], halo_recv.at[5], left)
    send(from_up.at[:, last], from_left.at[:, upper], halo_send.at[6], halo_recv.at[6], right)
    send(from_down.at[:, last], from_left.at[:, lower], halo_send.at[7], halo_recv.at[7], right)

    for part in range(2):
        for block in range(blocks):
            columns = pl.ds(block * s, s)
            new_copy_v[part, :, columns] = (
                w_v[part, block] - dual_v[part, :, columns] + (object_step * penalty) * cons_v[part, :, columns]
            )
        for block in range(1, last):
            columns = pl.ds(block * s, s)
            new_cons_v[part, middle, columns] = (
                w_v[part, block, middle] + (object_step * penalty) * cons_v[part, middle, columns]
            )
            new_dual_v[part, middle, columns] = jnp.zeros((tile_rows - s, s), F32)
    stores = [pltpu.make_async_copy(new_copy_v, new_copy_hbm, store_sems.at[0])]
    stores[0].start()

    def finish(span, block, total, own, cover_rows, inside_rows):
        columns = pl.ds(block * s, s)
        for part in range(2):
            summed = total(part)
            cover = cover_rows
            inside = inside_rows
            if block == 0:
                summed = summed + has_left * from_left[part, span]
                cover = cover * (1.0 + has_left)
            if block == last:
                summed = summed + has_right * from_right[part, span]
                cover = cover * (1.0 + has_right)
                inside = inside * has_right
            mean = summed * (1.0 / cover)
            new_dual_v[part, span, columns] = own(part) - inside * mean
            if block < last and own is not None and span is not lower:
                new_cons_v[part, span, columns] = mean + (object_step * penalty) * cons_v[part, span, columns]

    one = jnp.float32(1.0)

    def own_of(block, span):
        return lambda part: w_v[part, block, span]

    for block in range(1, last):
        finish(upper, block, lambda part: from_up[part, block], own_of(block, upper), 1.0 + has_up, one)
        finish(lower, block, lambda part: from_down[part, block], own_of(block, lower), 1.0 + has_down, has_down)
    received(2)
    received(3)
    for block in (0, last):
        finish(middle, block, own_of(block, middle), own_of(block, middle), one, one)
    for index in range(4):
        sent[corner + index].wait_recv()
    for block in (0, last):
        finish(upper, block, lambda part: from_up[part, block], own_of(block, upper), 1.0 + has_up, one)
        finish(lower, block, lambda part: from_down[part, block], own_of(block, lower), 1.0 + has_down, has_down)
    stores += [
        pltpu.make_async_copy(new_cons_v, new_cons_hbm, store_sems.at[1]),
        pltpu.make_async_copy(new_dual_v, new_dual_hbm, store_sems.at[2]),
    ]
    stores[1].start()
    stores[2].start()

    fast_arrived()
    power = jnp.zeros((share, s), F32)
    for index in range(fast):
        power = power + fast_all[index] * fast_all[index]
    rate = probe_step / jnp.sqrt(jnp.sum(power, keepdims=True) / (s * s) + epsilon)
    for index in range(fast):
        span = pl.ds(index * share, share)
        new_probe_ref[span, :] = probe_ref[span, :] - rate * fast_all[index]

    for move in sent:
        move.wait_send()
    for store in stores:
        store.wait()


def finish_step(n_row, n_col, local_copy, dual, gradient, consensus, halos, probe_grad, norm, probe):
    s = SIDE
    ext_rows, ext_cols = local_copy.shape[1:]
    tile_rows, tile_cols = consensus.shape[1:]
    blocks = ext_cols // s
    fast = min(FAST, n_col)
    slow = n_col // fast
    share = 2 * s // fast
    piece = share // slow
    vmem, hbm = pl.BlockSpec(memory_space=pltpu.VMEM), pl.BlockSpec(memory_space=pl.ANY)
    big = max(fast, slow, n_row)
    return pl.pallas_call(
        functools.partial(finish_body, n_row, n_col, fast, slow),
        in_specs=[hbm] * 7 + [vmem] * 3,
        out_specs=[hbm] * 3 + [vmem],
        out_shape=[
            jax.ShapeDtypeStruct(local_copy.shape, F32),
            jax.ShapeDtypeStruct(consensus.shape, F32),
            jax.ShapeDtypeStruct(local_copy.shape, F32),
            jax.ShapeDtypeStruct((2 * s, s), F32),
        ],
        scratch_shapes=[
            pltpu.VMEM(local_copy.shape, F32),
            pltpu.VMEM(local_copy.shape, F32),
            pltpu.VMEM((2, blocks, ext_rows, s), F32),
            pltpu.VMEM(local_copy.shape, F32),
            pltpu.VMEM((2, blocks, ext_rows, s), F32),
            pltpu.VMEM(local_copy.shape, F32),
            pltpu.VMEM(consensus.shape, F32),
            pltpu.VMEM(local_copy.shape, F32),
            pltpu.VMEM((2, blocks, s, s), F32),
            pltpu.VMEM((2, blocks, s, s), F32),
            pltpu.VMEM((2, ext_rows, s), F32),
            pltpu.VMEM((2, ext_rows, s), F32),
            pltpu.VMEM((fast, share + 8, s), F32),
            pltpu.VMEM((fast, share + 8, s), F32),
            pltpu.VMEM((slow, piece + 8, s), F32),
            pltpu.VMEM((slow, piece + 8, s), F32),
            pltpu.VMEM((piece + 8, s), F32),
            pltpu.VMEM((n_row, piece + 8, s), F32),
            pltpu.VMEM((slow, piece, s), F32),
            pltpu.VMEM((fast, share, s), F32),
            pltpu.SemaphoreType.DMA((7,)),
            pltpu.SemaphoreType.DMA((3,)),
            pltpu.SemaphoreType.DMA((8,)),
            pltpu.SemaphoreType.DMA((8,)),
            pltpu.SemaphoreType.DMA((5, big)),
            pltpu.SemaphoreType.DMA((5, big)),
        ],
        compiler_params=pltpu.CompilerParams(
            collective_id=0, has_side_effects=True, vmem_limit_bytes=50 * 2**20
        ),
        cost_estimate=pl.CostEstimate(flops=10**7, bytes_accessed=16 * 2**20, transcendentals=0),
    )(
        local_copy, dual, gradient, consensus, *halos,
        probe_grad.reshape(2 * s, s), norm, probe.reshape(2 * s, s),
    )


def per_device(n_row, n_col, local_copy, dual, consensus, probe, intensity, pos_rows, pos_cols):
    s = SIDE
    over = [(i * n_col + j, i, j) for i in range(n_row) for j in range(n_col)]
    from_below = lax.ppermute(consensus[:, :s, :], "row", [(i, i - 1) for i in range(1, n_row)])
    from_right = lax.ppermute(consensus[:, :, :s], "col", [(j, j - 1) for j in range(1, n_col)])
    from_both = lax.ppermute(
        consensus[:, :s, :s], ("row", "col"),
        [(index, index - n_col - 1) for index, i, j in over if i > 0 and j > 0],
    )
    gradient, probe_grad, norm = patch_gradients(pos_rows, pos_cols, local_copy, probe, intensity)
    new_copy, new_consensus, new_dual, new_probe = finish_step(
        n_row, n_col, local_copy, dual, gradient, consensus, (from_below, from_right, from_both),
        probe_grad, norm, probe,
    )
    return new_copy, new_consensus, new_dual, new_probe.reshape(probe.shape)


def solution(mesh):
    field = P(None, "row", "col")
    both = ("row", "col")
    return jax.shard_map(
        functools.partial(per_device, mesh.shape["row"], mesh.shape["col"]),
        mesh=mesh,
        in_specs=(field, field, field, P(), P(both, None, None), P(both), P(both)),
        out_specs=(field, field, field, P()),
        check_vma=False,
    )
```

```python
import functools
import math

import jax
import jax.numpy as jnp
import ml_dtypes
import numpy as np
from jax import lax
from jax.experimental import pallas as pl
from jax.experimental.pallas import tpu as pltpu
from jax.sharding import PartitionSpec as P

MESH = pl.DeviceIdType.MESH
F32 = jnp.float32
BF16 = jnp.bfloat16
SIDE = 128
BATCH = 8

object_step = 0.3
penalty = 1.0
probe_step = 0.5
epsilon = 1e-06


def dft_tables():
    index = np.arange(SIDE)
    angle = 2.0 * np.pi * ((index[:, None] * index[None, :]) % SIDE) / SIDE
    cosine = np.cos(angle) / math.sqrt(SIDE)
    sine = np.sin(angle) / math.sqrt(SIDE)
    forward = np.block([[cosine, -sine], [sine, cosine]])
    backward = np.block([[cosine, sine], [-sine, cosine]])
    parts = []
    for table in (forward, backward):
        high = table.astype(ml_dtypes.bfloat16)
        parts += [high, (table - high.astype(np.float64)).astype(ml_dtypes.bfloat16)]
    return np.stack(parts)


def halves(value):
    high = value.astype(BF16)
    return high, (value - high.astype(F32)).astype(BF16)


def times_right(value, high_table, low_table):
    high, low = halves(value)
    return jnp.dot(
        jnp.concatenate([high, low, high], 1),
        jnp.concatenate([high_table, high_table, low_table], 0),
        preferred_element_type=F32,
    )


def times_left(high_table, low_table, value):
    high, low = halves(value)
    return jnp.dot(
        jnp.concatenate([high_table, low_table, high_table], 1),
        jnp.concatenate([high, high, low], 0),
        preferred_element_type=F32,
    )


def swapped(value):
    s = SIDE
    return jnp.concatenate(
        [
            jnp.concatenate([value[:s, :s], value[s:, :s]], 1),
            jnp.concatenate([value[:s, s:], value[s:, s:]], 1),
        ],
        0,
    )


def patch_body(
    rows_hbm, cols_hbm, copy_hbm, probe_hbm, data_hbm, tables_hbm,
    grad_ref, probe_grad_ref, norm_ref,
    copy_ref, data_ref, rows_ref, cols_ref, probe_ref, tables_ref, sems,
):
    s = SIDE
    count = data_ref.shape[0]
    blocks, ext_rows = copy_ref.shape[1:3]
    tile_rows, tile_cols = ext_rows - s, (blocks - 1) * s
    moves = [
        pltpu.make_async_copy(rows_hbm, rows_ref, sems.at[0]),
        pltpu.make_async_copy(cols_hbm, cols_ref, sems.at[1]),
        pltpu.make_async_copy(probe_hbm, probe_ref, sems.at[2]),
        pltpu.make_async_copy(tables_hbm, tables_ref, sems.at[3]),
    ]
    for block in range(blocks):
        moves.append(
            pltpu.make_async_copy(
                copy_hbm.at[:, :, pl.ds(block * s, s)], copy_ref.at[:, block], sems.at[4 + block]
            )
        )
    for move in moves:
        move.start()

    def data_move(part):
        span = pl.ds(part * BATCH, BATCH)
        return pltpu.make_async_copy(data_hbm.at[span], data_ref.at[span], sems.at[4 + blocks + part])

    for part in range(count // BATCH):
        data_move(part).start()
    grad_ref[...] = jnp.zeros_like(grad_ref)
    probe_grad_ref[...] = jnp.zeros_like(probe_grad_ref)
    lane = lax.broadcasted_iota(jnp.int32, (s, s), 1)
    for move in moves:
        move.wait()

    def step(index, carry):
        data_move(index).wait()
        forward = (tables_ref[0], tables_ref[1])
        backward = (tables_ref[2], tables_ref[3])
        probe_re, probe_im = probe_ref[0], probe_ref[1]
        places, fields = [], []
        for member in range(BATCH):
            top = rows_ref[index * BATCH + member] & (tile_rows - 1)
            left = cols_ref[index * BATCH + member] & (tile_cols - 1)
            block, shift = left // s, left % s
            places.append((top, block, shift))
            field = []
            for part in range(2):
                near = copy_ref[part, block, pl.ds(top, s), :]
                far = copy_ref[part, block + 1, pl.ds(top, s), :]
                field.append(pltpu.roll(jnp.where(lane >= shift, near, far), (s - shift) % s, 1))
            fields.append(field)
        sum_re = jnp.zeros((s, s), F32)
        sum_im = jnp.zeros((s, s), F32)
        waves = []
        for first in range(0, BATCH, 2):
            wave = jnp.concatenate(
                [
                    jnp.concatenate(
                        [probe_re * re - probe_im * im, probe_re * im + probe_im * re], 1
                    )
                    for re, im in fields[first : first + 2]
                ],
                0,
            )
            waves.append(wave)
        rows_done = times_right(jnp.concatenate(waves, 0), *forward)
        misfits = []
        for first in range(0, BATCH, 2):
            spectrum = times_left(*backward, swapped(rows_done[first * s : (first + 2) * s]))
            spec_re, spec_im = spectrum[:s], spectrum[s:]
            data = jnp.concatenate(
                [data_ref[index * BATCH + first], data_ref[index * BATCH + first + 1]], 1
            )
            residue = spec_re * spec_re + spec_im * spec_im - data
            weighted = jnp.concatenate([residue * spec_re, residue * spec_im], 0)
            misfits.append(swapped(times_left(*forward, weighted)))
        misfit_all = times_right(jnp.concatenate(misfits, 0), *backward)
        for first in range(0, BATCH, 2):
            misfit = misfit_all[first * s : (first + 2) * s]
            for second in range(2):
                member = first + second
                mis_re = misfit[second * s : (second + 1) * s, :s]
                mis_im = misfit[second * s : (second + 1) * s, s:]
                re, im = fields[member]
                sum_re += re * mis_re + im * mis_im
                sum_im += re * mis_im - im * mis_re
                top, block, shift = places[member]
                terms = (probe_re * mis_re + probe_im * mis_im, probe_re * mis_im - probe_im * mis_re)
                for part in range(2):
                    term = pltpu.roll(terms[part], shift, 1)
                    grad_ref[part, block, pl.ds(top, s), :] += jnp.where(lane >= shift, term, 0.0)
                    grad_ref[part, block + 1, pl.ds(top, s), :] += jnp.where(lane >= shift, 0.0, term)
        probe_grad_ref[0] += sum_re
        probe_grad_ref[1] += sum_im
        return carry

    lax.fori_loop(0, count // BATCH, step, 0)

    def squares(index, total):
        for part in range(2):
            for block in range(blocks):
                value = grad_ref[part, block, pl.ds(pl.multiple_of(index * 8, 8), 8), :]
                total = total + value * value
        return total

    norm_ref[...] = lax.fori_loop(0, ext_rows // 8, squares, jnp.zeros((8, s), F32))


def patch_gradients(pos_rows, pos_cols, local_copy, probe, intensity):
    s = SIDE
    count = intensity.shape[0]
    ext_rows, ext_cols = local_copy.shape[1:]
    blocks = ext_cols // s
    vmem, hbm = pl.BlockSpec(memory_space=pltpu.VMEM), pl.BlockSpec(memory_space=pl.ANY)
    return pl.pallas_call(
        patch_body,
        in_specs=[hbm] * 6,
        out_specs=[vmem, vmem, vmem],
        out_shape=[
            jax.ShapeDtypeStruct((2, blocks, ext_rows, s), F32),
            jax.ShapeDtypeStruct((2, s, s), F32),
            jax.ShapeDtypeStruct((8, s), F32),
        ],
        scratch_shapes=[
            pltpu.VMEM((2, blocks, ext_rows, s), F32),
            pltpu.VMEM((count, s, s), F32),
            pltpu.SMEM(pos_rows.shape, jnp.int32),
            pltpu.SMEM(pos_cols.shape, jnp.int32),
            pltpu.VMEM(probe.shape, F32),
            pltpu.VMEM((4, 2 * s, 2 * s), BF16),
            pltpu.SemaphoreType.DMA((4 + blocks + count // BATCH,)),
        ],
        compiler_params=pltpu.CompilerParams(vmem_limit_bytes=50 * 2**20),
        cost_estimate=pl.CostEstimate(
            flops=count * 4 * 3 * 2 * s * 256 * 256, bytes_accessed=8 * 2**20, transcendentals=0
        ),
    )(pos_rows, pos_cols, local_copy, probe, intensity, jnp.asarray(dft_tables()))


def finish_body(
    n_row, n_col,
    copy_hbm, dual_hbm, grad_hbm, cons_hbm, left_hbm, probe_grad_ref, norm_ref, probe_ref,
    new_copy_ref, new_cons_ref, new_dual_ref, new_probe_ref,
    copy_v, dual_v, grad_v, cons_v, w_v,
    from_up, from_down, from_left, from_right,
    col_out, col_in, row_out, row_in, col_all,
    load_sems, halo_send, halo_recv, sum_send, sum_recv,
):
    s = SIDE
    a, b = lax.axis_index("row"), lax.axis_index("col")
    ext_rows, ext_cols = copy_v.shape[1:]
    tile_rows, tile_cols = ext_rows - s, ext_cols - s
    blocks = ext_cols // s
    last = blocks - 1
    lower, upper, middle = pl.ds(tile_rows, s), pl.ds(0, s), pl.ds(s, tile_rows - s)

    loads = []
    for index, (source, target) in enumerate(
        [
            (cons_hbm, cons_v.at[:, pl.ds(0, tile_rows), pl.ds(0, tile_cols)]),
            (left_hbm, cons_v.at[:, pl.ds(0, tile_rows), pl.ds(tile_cols, s)]),
            (copy_hbm, copy_v),
            (dual_hbm, dual_v),
            (grad_hbm, grad_v),
        ]
    ):
        loads.append(pltpu.make_async_copy(source, target, load_sems.at[index]))
        loads[-1].start()

    def row_peer(index):
        return (index, b)

    def col_peer(index):
        return (a, index)

    barrier = pltpu.get_barrier_semaphore()
    for peer, mine, size in ((row_peer, a, n_row), (col_peer, b, n_col)):

        def greet(hop, carry):
            pl.semaphore_signal(
                barrier, inc=1, device_id=peer(lax.rem(mine + hop, size)), device_id_type=MESH
            )
            return carry

        lax.fori_loop(1, size, greet, 0)
    pl.semaphore_wait(barrier, n_row + n_col - 2)

    def remote(source, target, send_sem, recv_sem, device):
        return pltpu.make_async_remote_copy(
            src_ref=source, dst_ref=target, send_sem=send_sem, recv_sem=recv_sem,
            device_id=device, device_id_type=MESH,
        )

    class Spread:
        def __init__(self, phase, peer, mine, size, source_of, slots):
            self.size = size

            def move(hop, other):
                return remote(
                    source_of(other), slots.at[mine], sum_send.at[phase, hop], sum_recv.at[phase, hop], peer(other)
                )

            def start(hop, carry):
                move(hop, lax.rem(mine + hop, size)).start()
                return carry

            def arrive(hop, carry):
                other = lax.rem(mine + size - hop, size)
                remote(
                    source_of(other), slots.at[other], sum_send.at[phase, hop], sum_recv.at[phase, hop], peer(other)
                ).wait_recv()
                return carry

            def leave(hop, carry):
                move(hop, lax.rem(mine + hop, size)).wait_send()
                return carry

            lax.fori_loop(1, size, start, 0)
            self.arrived = lambda: lax.fori_loop(1, size, arrive, 0)
            self.left = lambda: lax.fori_loop(1, size, leave, 0)

    class Halo:
        def __init__(self, index, source, target, sends, device, receives):
            move = remote(source, target, halo_send.at[index], halo_recv.at[index], device)
            self.move, self.sends, self.receives = move, sends, receives

        def start(self):
            pl.when(self.sends)(lambda: self.move.start())

        def arrived(self):
            pl.when(self.receives)(lambda: self.move.wait_recv())

        def left(self):
            pl.when(self.sends)(lambda: self.move.wait_send())

    up, down, left, right = (a - 1, b), (a + 1, b), (a, b - 1), (a, b + 1)
    is_up, is_down, is_left, is_right = a > 0, a < n_row - 1, b > 0, b < n_col - 1
    has_up, has_down = is_up.astype(F32), is_down.astype(F32)
    has_left, has_right = is_left.astype(F32), is_right.astype(F32)

    piece = col_out.shape[1] - 8
    for index in range(n_col):
        col_out[index, :piece] = probe_grad_ref[pl.ds(index * piece, piece), :]
        col_out[index, piece:] = norm_ref[...]
    first_sum = Spread(0, col_peer, b, n_col, lambda other: col_out.at[other], col_in)
    col_in[b] = col_out[b]

    cons_up = Halo(0, cons_v.at[:, upper], cons_v.at[:, lower], is_up, up, is_down)
    loads[0].wait()
    loads[1].wait()
    cons_up.start()
    pl.when(jnp.logical_not(is_down))(
        lambda: cons_v.__setitem__((slice(None), lower), jnp.zeros((2, s, ext_cols), F32))
    )

    first_sum.arrived()

    def total_of(slots, size):
        total = slots[0]
        for index in range(1, size):
            total = total + slots[index]
        return total

    row_out[...] = total_of(col_in, n_col)
    second_sum = Spread(1, row_peer, a, n_row, lambda other: row_out, row_in)
    row_in[a] = row_out[...]
    for load in loads[2:]:
        load.wait()
    second_sum.arrived()
    whole = total_of(row_in, n_row)
    squares = jnp.sum(whole[piece:], keepdims=True)
    scale = object_step / jnp.sqrt(squares / (n_row * n_col * ext_rows * ext_cols) + epsilon)
    keep = 1.0 - object_step * penalty
    pull = object_step * penalty

    def fill(first, count, block):
        columns = pl.ds(block * s, s)
        span = pl.ds(first, count)
        for part in range(2):
            old, dual = copy_v[part, span, columns], dual_v[part, span, columns]
            w_v[part, block, span, :] = keep * (old + dual) - scale * grad_v[part, block, span, :]

    rows_up = Halo(1, w_v.at[:, :, upper], from_down, is_up, up, is_down)
    rows_down = Halo(2, w_v.at[:, :, lower], from_up, is_down, down, is_up)
    mid_left = Halo(3, w_v.at[:, 0, middle], from_right.at[:, middle], is_left, left, is_right)
    mid_right = Halo(4, w_v.at[:, last, middle], from_left.at[:, middle], is_right, right, is_left)
    corners = [
        Halo(5, from_up.at[:, 0], from_right.at[:, upper], is_left, left, is_right),
        Halo(6, from_down.at[:, 0], from_right.at[:, lower], is_left, left, is_right),
        Halo(7, from_up.at[:, last], from_left.at[:, upper], is_right, right, is_left),
        Halo(8, from_down.at[:, last], from_left.at[:, lower], is_right, right, is_left),
    ]
    for block in range(blocks):
        fill(0, s, block)
    rows_up.start()
    for block in range(blocks):
        fill(tile_rows, s, block)
    rows_down.start()
    fill(s, tile_rows - s, 0)
    mid_left.start()
    fill(s, tile_rows - s, last)
    mid_right.start()
    for block in range(1, last):
        fill(s, tile_rows - s, block)

    col_all[b] = whole[:piece]
    third_sum = Spread(2, col_peer, b, n_col, lambda other: col_all.at[b], col_all)

    cons_up.arrived()
    for part in range(2):
        for block in range(blocks):
            columns = pl.ds(block * s, s)
            new_copy_ref[part, :, columns] = (
                w_v[part, block] - dual_v[part, :, columns] + pull * cons_v[part, :, columns]
            )
        for block in range(1, last):
            columns = pl.ds(block * s, s)
            new_cons_ref[part, middle, columns] = w_v[part, block, middle] + pull * cons_v[part, middle, columns]
            new_dual_ref[part, middle, columns] = jnp.zeros((tile_rows - s, s), F32)

    def neighbour(present, value):
        return jnp.where(present, value, 0.0)

    rows_up.arrived()
    rows_down.arrived()
    for part in range(2):
        for block in range(blocks):
            from_up[part, block] = w_v[part, block, upper] + neighbour(is_up, from_up[part, block])
            from_down[part, block] = w_v[part, block, lower] + neighbour(is_down, from_down[part, block])
    for corner in corners:
        corner.start()

    def finish(span, block, total, cover_rows, inside_rows):
        columns = pl.ds(block * s, s)
        for part in range(2):
            summed = total(part)
            cover = cover_rows
            inside = inside_rows
            if block == 0:
                summed = summed + neighbour(is_left, from_left[part, span])
                cover = cover * (1.0 + has_left)
            if block == last:
                summed = summed + neighbour(is_right, from_right[part, span])
                cover = cover * (1.0 + has_right)
                inside = inside * has_right
            mean = summed * (1.0 / cover)
            new_dual_ref[part, span, columns] = w_v[part, block, span] - inside * mean
            if block < last and span is not lower:
                new_cons_ref[part, span, columns] = mean + pull * cons_v[part, span, columns]

    one = jnp.float32(1.0)

    def top_and_bottom(block):
        finish(upper, block, lambda part: from_up[part, block], 1.0 + has_up, one)
        finish(lower, block, lambda part: from_down[part, block], 1.0 + has_down, has_down)

    for block in range(1, last):
        top_and_bottom(block)
    mid_left.arrived()
    mid_right.arrived()
    for block in (0, last):
        finish(middle, block, lambda part: w_v[part, block, middle], one, one)

    third_sum.arrived()
    power = jnp.zeros((piece, s), F32)
    for index in range(n_col):
        power = power + col_all[index] * col_all[index]
    rate = probe_step / jnp.sqrt(jnp.sum(power, keepdims=True) / (s * s) + epsilon)
    for index in range(n_col):
        span = pl.ds(index * piece, piece)
        new_probe_ref[span, :] = probe_ref[span, :] - rate * col_all[index]

    for corner in corners:
        corner.arrived()
    for block in (0, last):
        top_and_bottom(block)

    for move in [cons_up, rows_up, rows_down, mid_left, mid_right] + corners + [first_sum, second_sum, third_sum]:
        move.left()


def finish_step(n_row, n_col, local_copy, dual, gradient, consensus, beside, probe_grad, norm, probe):
    s = SIDE
    ext_rows, ext_cols = local_copy.shape[1:]
    blocks = ext_cols // s
    piece = 2 * s // n_col
    vmem, hbm = pl.BlockSpec(memory_space=pltpu.VMEM), pl.BlockSpec(memory_space=pl.ANY)
    return pl.pallas_call(
        functools.partial(finish_body, n_row, n_col),
        in_specs=[hbm] * 5 + [vmem] * 3,
        out_specs=[vmem] * 4,
        out_shape=[
            jax.ShapeDtypeStruct(local_copy.shape, F32),
            jax.ShapeDtypeStruct(consensus.shape, F32),
            jax.ShapeDtypeStruct(local_copy.shape, F32),
            jax.ShapeDtypeStruct((2 * s, s), F32),
        ],
        scratch_shapes=[
            pltpu.VMEM(local_copy.shape, F32),
            pltpu.VMEM(local_copy.shape, F32),
            pltpu.VMEM((2, blocks, ext_rows, s), F32),
            pltpu.VMEM(local_copy.shape, F32),
            pltpu.VMEM((2, blocks, ext_rows, s), F32),
            pltpu.VMEM((2, blocks, s, s), F32),
            pltpu.VMEM((2, blocks, s, s), F32),
            pltpu.VMEM((2, ext_rows, s), F32),
            pltpu.VMEM((2, ext_rows, s), F32),
            pltpu.VMEM((n_col, piece + 8, s), F32),
            pltpu.VMEM((n_col, piece + 8, s), F32),
            pltpu.VMEM((piece + 8, s), F32),
            pltpu.VMEM((n_row, piece + 8, s), F32),
            pltpu.VMEM((n_col, piece, s), F32),
            pltpu.SemaphoreType.DMA((5,)),
            pltpu.SemaphoreType.DMA((9,)),
            pltpu.SemaphoreType.DMA((9,)),
            pltpu.SemaphoreType.DMA((3, max(n_row, n_col))),
            pltpu.SemaphoreType.DMA((3, max(n_row, n_col))),
        ],
        compiler_params=pltpu.CompilerParams(
            collective_id=0, has_side_effects=True, vmem_limit_bytes=32 * 2**20
        ),
        cost_estimate=pl.CostEstimate(flops=10**7, bytes_accessed=16 * 2**20, transcendentals=0),
    )(
        local_copy, dual, gradient, consensus, beside,
        probe_grad.reshape(2 * s, s), norm, probe.reshape(2 * s, s),
    )


def store_body(*refs):
    count = len(refs) // 2
    sources, targets, sems = refs[:count], refs[count : 2 * count], refs[2 * count]
    moves = [
        pltpu.make_async_copy(source.at[part], target.at[part], sems.at[index, part])
        for index, (source, target) in enumerate(zip(sources, targets))
        for part in range(2)
    ]
    for move in moves:
        move.start()
    for move in moves:
        move.wait()


def store(*arrays):
    return pl.pallas_call(
        store_body,
        in_specs=[pl.BlockSpec(memory_space=pltpu.VMEM)] * len(arrays),
        out_specs=[pl.BlockSpec(memory_space=pl.ANY)] * len(arrays),
        out_shape=[jax.ShapeDtypeStruct(array.shape, F32) for array in arrays],
        scratch_shapes=[pltpu.SemaphoreType.DMA((len(arrays), 2))],
        compiler_params=pltpu.CompilerParams(vmem_limit_bytes=16 * 2**20),
    )(*arrays)


def per_device(n_row, n_col, local_copy, dual, consensus, probe, intensity, pos_rows, pos_cols):
    s = SIDE
    beside = lax.ppermute(consensus[:, :, :s], "col", [(j, j - 1) for j in range(1, n_col)])
    gradient, probe_grad, norm = patch_gradients(pos_rows, pos_cols, local_copy, probe, intensity)
    new_copy, new_consensus, new_dual, new_probe = finish_step(
        n_row, n_col, local_copy, dual, gradient, consensus, beside, probe_grad, norm, probe
    )
    return tuple(store(new_copy, new_consensus, new_dual, new_probe.reshape(probe.shape)))


def solution(mesh):
    field = P(None, "row", "col")
    both = ("row", "col")
    return jax.shard_map(
        functools.partial(per_device, mesh.shape["row"], mesh.shape["col"]),
        mesh=mesh,
        in_specs=(field, field, field, P(), P(both, None, None), P(both), P(both)),
        out_specs=(field, field, field, P()),
        check_vma=False,
    )
```

```python
import functools
import math

import jax
import jax.numpy as jnp
import ml_dtypes
import numpy as np
from jax import lax
from jax.experimental import pallas as pl
from jax.experimental.pallas import tpu as pltpu
from jax.sharding import PartitionSpec as P

MESH = pl.DeviceIdType.MESH
F32 = jnp.float32
BF16 = jnp.bfloat16
SIDE = 128
BATCH = 8

object_step = 0.3
penalty = 1.0
probe_step = 0.5
epsilon = 1e-06


def dft_tables():
    index = np.arange(SIDE)
    angle = 2.0 * np.pi * ((index[:, None] * index[None, :]) % SIDE) / SIDE
    cosine = np.cos(angle) / math.sqrt(SIDE)
    sine = np.sin(angle) / math.sqrt(SIDE)
    forward = np.block([[cosine, -sine], [sine, cosine]])
    backward = np.block([[cosine, sine], [-sine, cosine]])
    parts = []
    for table in (forward, backward):
        high = table.astype(ml_dtypes.bfloat16)
        parts += [high, (table - high.astype(np.float64)).astype(ml_dtypes.bfloat16)]
    return np.stack(parts)


def halves(value):
    high = value.astype(BF16)
    return high, (value - high.astype(F32)).astype(BF16)


def times_right(value, high_table, low_table):
    high, low = halves(value)
    return jnp.dot(
        jnp.concatenate([high, low, high], 1),
        jnp.concatenate([high_table, high_table, low_table], 0),
        preferred_element_type=F32,
    )


def times_left(high_table, low_table, value):
    high, low = halves(value)
    return jnp.dot(
        jnp.concatenate([high_table, low_table, high_table], 1),
        jnp.concatenate([high, high, low], 0),
        preferred_element_type=F32,
    )


def swapped(value):
    s = SIDE
    return jnp.concatenate(
        [
            jnp.concatenate([value[:s, :s], value[s:, :s]], 1),
            jnp.concatenate([value[:s, s:], value[s:, s:]], 1),
        ],
        0,
    )


def step_body(
    n_row, n_col,
    rows_hbm, cols_hbm, copy_hbm, dual_hbm, cons_hbm, probe_hbm, data_hbm, tables_hbm,
    new_copy_ref, new_cons_ref, new_dual_ref, new_probe_ref,
    rows_ref, cols_ref, copy_v, dual_v, cons_v, probe_v, data_v, tables_v,
    terms_v, grad_v, probe_grad_v, w_v,
    from_up, from_down, from_left, from_right,
    col_out, col_in, row_out, row_in, col_all,
    load_sems, halo_send, halo_recv, sum_send, sum_recv,
):
    s = SIDE
    a, b = lax.axis_index("row"), lax.axis_index("col")
    blocks, ext_rows = copy_v.shape[1:3]
    ext_cols = blocks * s
    tile_rows, tile_cols = ext_rows - s, ext_cols - s
    count = data_v.shape[0]
    last = blocks - 1
    lower, upper, middle = pl.ds(tile_rows, s), pl.ds(0, s), pl.ds(s, tile_rows - s)

    pairs = [
        (rows_hbm, rows_ref),
        (cols_hbm, cols_ref),
        (probe_hbm, probe_v),
        (tables_hbm, tables_v),
    ]
    for block in range(blocks):
        pairs.append((copy_hbm.at[:, :, pl.ds(block * s, s)], copy_v.at[:, block]))
    needed = len(pairs)
    for part in range(count // BATCH):
        span = pl.ds(part * BATCH, BATCH)
        pairs.append((data_hbm.at[span], data_v.at[span]))
    early = len(pairs) - count // BATCH + 1
    for block in range(last):
        pairs.append((cons_hbm.at[:, :, pl.ds(block * s, s)], cons_v.at[:, block, pl.ds(0, tile_rows)]))
    pairs.append((dual_hbm, dual_v))
    loads = [
        pltpu.make_async_copy(source, target, load_sems.at[index])
        for index, (source, target) in enumerate(pairs)
    ]
    for load in loads[:early] + loads[-1 - last : -1]:
        load.start()

    def row_peer(index):
        return (index, b)

    def col_peer(index):
        return (a, index)

    barrier = pltpu.get_barrier_semaphore()
    for peer, mine, size in ((row_peer, a, n_row), (col_peer, b, n_col)):

        def greet(hop, carry):
            pl.semaphore_signal(
                barrier, inc=1, device_id=peer(lax.rem(mine + hop, size)), device_id_type=MESH
            )
            return carry

        lax.fori_loop(1, size, greet, 0)

    terms_v[...] = jnp.zeros_like(terms_v)
    grad_v[...] = jnp.zeros_like(grad_v)
    probe_grad_v[...] = jnp.zeros_like(probe_grad_v)

    def remote(source, target, send_sem, recv_sem, device):
        return pltpu.make_async_remote_copy(
            src_ref=source, dst_ref=target, send_sem=send_sem, recv_sem=recv_sem,
            device_id=device, device_id_type=MESH,
        )

    class Spread:
        def __init__(self, phase, peer, mine, size, source_of, slots):
            def move(hop, other):
                return remote(
                    source_of(other), slots.at[mine], sum_send.at[phase, hop], sum_recv.at[phase, hop], peer(other)
                )

            def start(hop, carry):
                move(hop, lax.rem(mine + hop, size)).start()
                return carry

            def arrive(hop, carry):
                other = lax.rem(mine + size - hop, size)
                remote(
                    source_of(other), slots.at[other], sum_send.at[phase, hop], sum_recv.at[phase, hop], peer(other)
                ).wait_recv()
                return carry

            def leave(hop, carry):
                move(hop, lax.rem(mine + hop, size)).wait_send()
                return carry

            lax.fori_loop(1, size, start, 0)
            self.arrived = lambda: lax.fori_loop(1, size, arrive, 0)
            self.left = lambda: lax.fori_loop(1, size, leave, 0)

    class Halo:
        def __init__(self, index, source, target, sends, device, receives):
            move = remote(source, target, halo_send.at[index], halo_recv.at[index], device)
            self.move, self.sends, self.receives = move, sends, receives

        def start(self):
            pl.when(self.sends)(lambda: self.move.start())

        def arrived(self):
            pl.when(self.receives)(lambda: self.move.wait_recv())

        def left(self):
            pl.when(self.sends)(lambda: self.move.wait_send())

    up, down, left, right = (a - 1, b), (a + 1, b), (a, b - 1), (a, b + 1)
    is_up, is_down, is_left, is_right = a > 0, a < n_row - 1, b > 0, b < n_col - 1
    has_up, has_down = is_up.astype(F32), is_down.astype(F32)
    has_left, has_right = is_left.astype(F32), is_right.astype(F32)
    own_rows = pl.ds(0, tile_rows)
    cons_left = Halo(
        0, cons_v.at[:, 0, own_rows], cons_v.at[:, last, own_rows], is_left, left, is_right
    )
    inner = pl.ds(0, last)
    cons_up = Halo(1, cons_v.at[:, inner, upper], cons_v.at[:, inner, lower], is_up, up, is_down)
    cons_corner = Halo(2, cons_v.at[:, last, upper], cons_v.at[:, last, lower], is_up, up, is_down)

    lane = lax.broadcasted_iota(jnp.int32, (s, s), 1)

    def place(member):
        top = rows_ref[member] & (tile_rows - 1)
        left_col = cols_ref[member] & (tile_cols - 1)
        return top, left_col // s, left_col % s

    def collect(batch):
        spots = [place(batch * BATCH + member) for member in range(BATCH)]
        for first in range(0, ext_rows, s):
            span = pl.ds(first, s)
            rows = [jnp.clip(first - top, -s, s) + s for top, _, _ in spots]
            for part in range(2):
                for block in range(blocks):
                    total = grad_v[part, block, span, :]
                    for member in range(BATCH):
                        _, home, _ = spots[member]
                        kind = jnp.clip(block - home, 0, 1)
                        row = jnp.where(kind == block - home, rows[member], 0)
                        total = total + terms_v[kind, member, part, pl.ds(row, s), :]
                    grad_v[part, block, span, :] = total

    for load in loads[:needed]:
        load.wait()
    for load in loads[early : early + count // BATCH - 1] + loads[-1:]:
        load.start()

    def work(index, carry):
        loads_data(index).wait()

        collect(jnp.maximum(index - 1, 0))

        @pl.when(index == 1)
        def _():
            pl.semaphore_wait(barrier, n_row + n_col - 2)
            for load in loads[-1 - last : -1]:
                load.wait()
            cons_up.start()
            cons_left.start()

        forward = (tables_v[0], tables_v[1])
        backward = (tables_v[2], tables_v[3])
        probe_re, probe_im = probe_v[0], probe_v[1]
        spots, fields = [], []
        for member in range(BATCH):
            top, block, shift = place(index * BATCH + member)
            spots.append(shift)
            field = []
            for part in range(2):
                near = copy_v[part, block, pl.ds(top, s), :]
                far = copy_v[part, block + 1, pl.ds(top, s), :]
                field.append(pltpu.roll(jnp.where(lane >= shift, near, far), (s - shift) % s, 1))
            fields.append(field)
        sum_re = jnp.zeros((s, s), F32)
        sum_im = jnp.zeros((s, s), F32)
        waves = []
        for re, im in fields:
            waves.append(
                jnp.concatenate([probe_re * re - probe_im * im, probe_re * im + probe_im * re], 1)
            )
        rows_done = times_right(jnp.concatenate(waves, 0), *forward)
        misfits = []
        for first in range(0, BATCH, 2):
            spectrum = times_left(*backward, swapped(rows_done[first * s : (first + 2) * s]))
            spec_re, spec_im = spectrum[:s], spectrum[s:]
            data = jnp.concatenate(
                [data_v[index * BATCH + first], data_v[index * BATCH + first + 1]], 1
            )
            residue = spec_re * spec_re + spec_im * spec_im - data
            weighted = jnp.concatenate([residue * spec_re, residue * spec_im], 0)
            misfits.append(swapped(times_left(*forward, weighted)))
        misfit = times_right(jnp.concatenate(misfits, 0), *backward)
        for member in range(BATCH):
            mis_re = misfit[member * s : (member + 1) * s, :s]
            mis_im = misfit[member * s : (member + 1) * s, s:]
            re, im = fields[member]
            sum_re += re * mis_re + im * mis_im
            sum_im += re * mis_im - im * mis_re
            shift = spots[member]
            terms = (probe_re * mis_re + probe_im * mis_im, probe_re * mis_im - probe_im * mis_re)
            for part in range(2):
                term = pltpu.roll(terms[part], shift, 1)
                terms_v[0, member, part, pl.ds(s, s), :] = jnp.where(lane >= shift, term, 0.0)
                terms_v[1, member, part, pl.ds(s, s), :] = jnp.where(lane >= shift, 0.0, term)
        probe_grad_v[0] += sum_re
        probe_grad_v[1] += sum_im
        return carry

    def loads_data(index):
        span = pl.ds(index * BATCH, BATCH)
        return pltpu.make_async_copy(data_hbm.at[span], data_v.at[span], load_sems.at[needed + index])

    lax.fori_loop(0, count // BATCH, work, 0)
    collect(count // BATCH - 1)

    def squares(index, total):
        for part in range(2):
            for block in range(blocks):
                value = grad_v[part, block, pl.ds(pl.multiple_of(index * 8, 8), 8), :]
                total = total + value * value
        return total

    norm = lax.fori_loop(0, ext_rows // 8, squares, jnp.zeros((8, s), F32))

    piece = col_out.shape[1] - 8
    for index in range(n_col):
        first = index * piece
        col_out[index, :piece] = probe_grad_v[first // s, pl.ds(first % s, piece), :]
        col_out[index, piece:] = norm
    first_sum = Spread(0, col_peer, b, n_col, lambda other: col_out.at[other], col_in)
    col_in[b] = col_out[b]

    loads[-1].wait()

    first_sum.arrived()

    def total_of(slots, size):
        total = slots[0]
        for index in range(1, size):
            total = total + slots[index]
        return total

    row_out[...] = total_of(col_in, n_col)
    second_sum = Spread(1, row_peer, a, n_row, lambda other: row_out, row_in)
    row_in[a] = row_out[...]
    second_sum.arrived()
    whole = total_of(row_in, n_row)
    total_squares = jnp.sum(whole[piece:], keepdims=True)
    scale = object_step / jnp.sqrt(total_squares / (n_row * n_col * ext_rows * ext_cols) + epsilon)
    keep = 1.0 - object_step * penalty
    pull = object_step * penalty

    def fill(first, size, block):
        columns = pl.ds(block * s, s)
        span = pl.ds(first, size)
        for part in range(2):
            old, dual = copy_v[part, block, span], dual_v[part, span, columns]
            w_v[part, block, span, :] = keep * (old + dual) - scale * grad_v[part, block, span, :]

    order = [(part, block) for block in [0, last] + list(range(1, last)) for part in range(2)]
    rows_up, rows_down = {}, {}
    for index, (part, block) in enumerate(order):
        rows_up[part, block] = Halo(
            3 + index, w_v.at[part, block, upper], from_down.at[part, block], is_up, up, is_down
        )
        rows_down[part, block] = Halo(
            3 + len(order) + index, w_v.at[part, block, lower], from_up.at[part, block], is_down, down, is_up
        )
    used = 3 + 2 * len(order)
    half, edge = n_col // 2, n_col - 1
    via_last, via_first = (b == half) & (n_col > 2), (b == half - 1) & (n_col > 2)
    mids = [
        Halo(used, w_v.at[0, 0, middle], from_right.at[0, middle], is_left, left, is_right),
        Halo(used + 1, w_v.at[0, last, middle], from_left.at[0, middle], is_right, right, is_left),
        Halo(
            used + 2, w_v.at[1, 0, middle], from_right.at[1, middle],
            is_left, (a, jnp.where(via_last, edge, b - 1)), is_right,
        ),
        Halo(
            used + 3, w_v.at[1, last, middle], from_left.at[1, middle],
            is_right, (a, jnp.where(via_first, 0, b + 1)), is_left,
        ),
    ]
    passed = [
        Halo(used + 2, from_right.at[1, middle], from_right.at[1, middle], b == edge, (a, half - 1), False),
        Halo(used + 3, from_left.at[1, middle], from_left.at[1, middle], b == 0, (a, half), False),
    ]
    used += 4
    corners = {}
    for part in range(2):
        for block, target, sends, device, receives in (
            (0, from_right, is_left, left, is_right),
            (last, from_left, is_right, right, is_left),
        ):
            for source, span in ((from_up, upper), (from_down, lower)):
                corners[part, block, span is upper] = Halo(
                    used, source.at[part, block], target.at[part, span], sends, device, receives
                )
                used += 1
    col_all[b] = whole[:piece]
    third_sum = Spread(2, col_peer, b, n_col, lambda other: col_all.at[b], col_all)
    for block in (0, last):
        fill(0, s, block)
        fill(tile_rows, s, block)
        for part in range(2):
            rows_up[part, block].start()
            rows_down[part, block].start()
    fill(s, tile_rows - s, 0)
    mids[2].start()
    mids[0].start()
    fill(s, tile_rows - s, last)
    mids[3].start()
    mids[1].start()
    for block in range(1, last):
        fill(0, s, block)
        fill(tile_rows, s, block)
        for part in range(2):
            rows_up[part, block].start()
            rows_down[part, block].start()
    for block in range(1, last):
        fill(s, tile_rows - s, block)

    def neighbour(present, value):
        return jnp.where(present, value, 0.0)

    def join(part, block):
        rows_up[part, block].arrived()
        rows_down[part, block].arrived()
        from_up[part, block] = w_v[part, block, upper] + neighbour(is_up, from_up[part, block])
        from_down[part, block] = w_v[part, block, lower] + neighbour(is_down, from_down[part, block])

    for block in (0, last):
        for part in range(2):
            join(part, block)
            corners[part, block, True].start()
            corners[part, block, False].start()

    if n_col > 2:
        for flag, move, onward in ((b == edge, mids[2], passed[0]), (b == 0, mids[3], passed[1])):

            @pl.when(flag)
            def _():
                move.move.wait_recv()
                onward.move.start()

    cons_left.arrived()
    pl.when(jnp.logical_not(is_right))(
        lambda: cons_v.__setitem__((slice(None), last, own_rows), jnp.zeros((2, tile_rows, s), F32))
    )
    cons_corner.start()
    pl.when(jnp.logical_not(is_down))(
        lambda: cons_v.__setitem__((slice(None), slice(None), lower), jnp.zeros((2, blocks, s, s), F32))
    )
    cons_up.arrived()

    def renew(span, block):
        columns = pl.ds(block * s, s)
        for part in range(2):
            new_copy_ref[part, span, columns] = (
                w_v[part, block, span] - dual_v[part, span, columns] + pull * cons_v[part, block, span]
            )

    for block in range(blocks):
        renew(own_rows, block)
        if block < last:
            renew(lower, block)
    for part in range(2):
        for block in range(1, last):
            columns = pl.ds(block * s, s)
            new_cons_ref[part, middle, columns] = w_v[part, block, middle] + pull * cons_v[part, block, middle]
            new_dual_ref[part, middle, columns] = jnp.zeros((tile_rows - s, s), F32)

    def finish(span, block, total, cover_rows, inside_rows):
        columns = pl.ds(block * s, s)
        for part in range(2):
            summed = total(part)
            cover = cover_rows
            inside = inside_rows
            if block == 0:
                summed = summed + neighbour(is_left, from_left[part, span])
                cover = cover * (1.0 + has_left)
            if block == last:
                summed = summed + neighbour(is_right, from_right[part, span])
                cover = cover * (1.0 + has_right)
                inside = inside * has_right
            mean = summed * (1.0 / cover)
            new_dual_ref[part, span, columns] = w_v[part, block, span] - inside * mean
            if block < last and span is not lower:
                new_cons_ref[part, span, columns] = mean + pull * cons_v[part, block, span]

    one = jnp.float32(1.0)

    def top_and_bottom(block):
        finish(upper, block, lambda part: from_up[part, block], 1.0 + has_up, one)
        finish(lower, block, lambda part: from_down[part, block], 1.0 + has_down, has_down)

    for block in range(1, last):
        for part in range(2):
            join(part, block)
        top_and_bottom(block)
    mids[0].arrived()
    mids[1].arrived()
    mids[2].arrived()
    mids[3].arrived()
    for block in (0, last):
        finish(middle, block, lambda part: w_v[part, block, middle], one, one)

    third_sum.arrived()
    power = jnp.zeros((piece, s), F32)
    for index in range(n_col):
        power = power + col_all[index] * col_all[index]
    rate = probe_step / jnp.sqrt(jnp.sum(power, keepdims=True) / (s * s) + epsilon)
    for index in range(n_col):
        first = index * piece
        half, span = first // s, pl.ds(first % s, piece)
        new_probe_ref[half, span, :] = probe_v[half, span, :] - rate * col_all[index]

    cons_corner.arrived()
    renew(lower, last)
    for corner in corners.values():
        corner.arrived()
    for block in (0, last):
        top_and_bottom(block)

    halos = [cons_left, cons_up, cons_corner] + mids + (passed if n_col > 2 else [])
    for group in (rows_up, rows_down, corners):
        halos += list(group.values())
    for move in halos + [first_sum, second_sum, third_sum]:
        move.left()


def step(n_row, n_col, pos_rows, pos_cols, local_copy, dual, consensus, probe, intensity):
    s = SIDE
    count = intensity.shape[0]
    ext_rows, ext_cols = local_copy.shape[1:]
    blocks = ext_cols // s
    piece = 2 * s // n_col
    vmem, hbm = pl.BlockSpec(memory_space=pltpu.VMEM), pl.BlockSpec(memory_space=pltpu.HBM)
    halos = 3 + 4 * blocks + 4 + 8
    return pl.pallas_call(
        functools.partial(step_body, n_row, n_col),
        in_specs=[hbm] * 8,
        out_specs=[vmem] * 4,
        out_shape=[
            jax.ShapeDtypeStruct(local_copy.shape, F32),
            jax.ShapeDtypeStruct(consensus.shape, F32),
            jax.ShapeDtypeStruct(local_copy.shape, F32),
            jax.ShapeDtypeStruct(probe.shape, F32),
        ],
        scratch_shapes=[
            pltpu.SMEM(pos_rows.shape, jnp.int32),
            pltpu.SMEM(pos_cols.shape, jnp.int32),
            pltpu.VMEM((2, blocks, ext_rows, s), F32),
            pltpu.VMEM(dual.shape, F32),
            pltpu.VMEM((2, blocks, ext_rows, s), F32),
            pltpu.VMEM(probe.shape, F32),
            pltpu.VMEM(intensity.shape, F32),
            pltpu.VMEM((4, 2 * s, 2 * s), BF16),
            pltpu.VMEM((2, BATCH, 2, 3 * s, s), F32),
            pltpu.VMEM((2, blocks, ext_rows, s), F32),
            pltpu.VMEM((2, s, s), F32),
            pltpu.VMEM((2, blocks, ext_rows, s), F32),
            pltpu.VMEM((2, blocks, s, s), F32),
            pltpu.VMEM((2, blocks, s, s), F32),
            pltpu.VMEM((2, ext_rows, s), F32),
            pltpu.VMEM((2, ext_rows, s), F32),
            pltpu.VMEM((n_col, piece + 8, s), F32),
            pltpu.VMEM((n_col, piece + 8, s), F32),
            pltpu.VMEM((piece + 8, s), F32),
            pltpu.VMEM((n_row, piece + 8, s), F32),
            pltpu.VMEM((n_col, piece, s), F32),
            pltpu.SemaphoreType.DMA((4 + blocks + count // BATCH + blocks,)),
            pltpu.SemaphoreType.DMA((halos,)),
            pltpu.SemaphoreType.DMA((halos,)),
            pltpu.SemaphoreType.DMA((3, max(n_row, n_col))),
            pltpu.SemaphoreType.DMA((3, max(n_row, n_col))),
        ],
        compiler_params=pltpu.CompilerParams(
            collective_id=0, has_side_effects=True, vmem_limit_bytes=46 * 2**20
        ),
        cost_estimate=pl.CostEstimate(
            flops=count * 4 * 3 * 2 * s * 256 * 256, bytes_accessed=16 * 2**20, transcendentals=0
        ),
    )(pos_rows, pos_cols, local_copy, dual, consensus, probe, intensity, jnp.asarray(dft_tables()))


def store_body(*refs):
    count = len(refs) // 2
    sources, targets, sems = refs[:count], refs[count : 2 * count], refs[2 * count]
    moves = [
        pltpu.make_async_copy(source.at[part], target.at[part], sems.at[index, part])
        for index, (source, target) in enumerate(zip(sources, targets))
        for part in range(2)
    ]
    for move in moves:
        move.start()
    for move in moves:
        move.wait()


def store(*arrays):
    return pl.pallas_call(
        store_body,
        in_specs=[pl.BlockSpec(memory_space=pltpu.VMEM)] * len(arrays),
        out_specs=[pl.BlockSpec(memory_space=pl.ANY)] * len(arrays),
        out_shape=[jax.ShapeDtypeStruct(array.shape, F32) for array in arrays],
        scratch_shapes=[pltpu.SemaphoreType.DMA((len(arrays), 2))],
        compiler_params=pltpu.CompilerParams(vmem_limit_bytes=16 * 2**20),
    )(*arrays)


def per_device(n_row, n_col, local_copy, dual, consensus, probe, intensity, pos_rows, pos_cols):
    new_copy, new_consensus, new_dual, new_probe = step(
        n_row, n_col, pos_rows, pos_cols, local_copy, dual, consensus, probe, intensity
    )
    return tuple(store(new_copy, new_consensus, new_dual, new_probe))


def solution(mesh):
    field = P(None, "row", "col")
    both = ("row", "col")
    return jax.shard_map(
        functools.partial(per_device, mesh.shape["row"], mesh.shape["col"]),
        mesh=mesh,
        in_specs=(field, field, field, P(), P(both, None, None), P(both), P(both)),
        out_specs=(field, field, field, P()),
        check_vma=False,
    )
```

```python
import functools
import math

import jax
import jax.numpy as jnp
from jax import lax
from jax.experimental import pallas as pl
from jax.experimental.pallas import tpu as pltpu
from jax.sharding import PartitionSpec as P

MESH = pl.DeviceIdType.MESH
F32 = jnp.float32
BF16 = jnp.bfloat16
SIDE = 128
BATCH = 8

object_step = 0.3
penalty = 1.0
probe_step = 0.5
epsilon = 1e-06


def fill_tables(tables_ref):
    row = lax.broadcasted_iota(jnp.int32, (SIDE, SIDE), 0)
    column = lax.broadcasted_iota(jnp.int32, (SIDE, SIDE), 1)
    turn = ((row * column + SIDE // 2) & (SIDE - 1)) - SIDE // 2
    angle = turn.astype(F32) * (math.pi / SIDE)
    square = angle * angle
    half_sine, half_cosine = jnp.zeros_like(angle), jnp.zeros_like(angle)
    for order in range(8, -1, -1):
        half_sine = half_sine * square + (-1.0) ** order / math.factorial(2 * order + 1)
        half_cosine = half_cosine * square + (-1.0) ** order / math.factorial(2 * order)
    half_sine = half_sine * angle
    norm = 1.0 / math.sqrt(SIDE)
    cosine = norm - (2.0 * norm) * half_sine * half_sine
    sine = (2.0 * norm) * half_sine * half_cosine
    for index, signed in enumerate((sine, -sine)):
        table = jnp.concatenate([jnp.concatenate([cosine, -signed], 1), jnp.concatenate([signed, cosine], 1)], 0)
        high, low = halves(table)
        tables_ref[2 * index] = high
        tables_ref[2 * index + 1] = low


def halves(value):
    high = value.astype(BF16)
    return high, (value - high.astype(F32)).astype(BF16)


def times_right(value, high_table, low_table):
    high, low = halves(value)
    return jnp.dot(
        jnp.concatenate([high, low, high], 1),
        jnp.concatenate([high_table, high_table, low_table], 0),
        preferred_element_type=F32,
    )


def times_left(high_table, low_table, value):
    high, low = halves(value)
    return jnp.dot(
        jnp.concatenate([high_table, low_table, high_table], 1),
        jnp.concatenate([high, high, low], 0),
        preferred_element_type=F32,
    )


def swapped(value):
    s = SIDE
    return jnp.concatenate(
        [
            jnp.concatenate([value[:s, :s], value[s:, :s]], 1),
            jnp.concatenate([value[:s, s:], value[s:, s:]], 1),
        ],
        0,
    )


def step_body(
    n_row, n_col,
    rows_hbm, cols_hbm, copy_hbm, dual_hbm, cons_hbm, probe_hbm, data_hbm,
    new_copy_ref, new_cons_ref, new_dual_ref, new_probe_ref,
    rows_ref, cols_ref, copy_v, dual_v, cons_v, probe_v, data_v, tables_v,
    terms_v, grad_v, probe_grad_v, w_v,
    from_up, from_down, from_left, from_right,
    col_out, col_in, row_out, row_in, col_all,
    load_sems, halo_send, halo_recv, sum_send, sum_recv,
):
    s = SIDE
    a, b = lax.axis_index("row"), lax.axis_index("col")
    blocks, ext_rows = copy_v.shape[1:3]
    ext_cols = blocks * s
    tile_rows, tile_cols = ext_rows - s, ext_cols - s
    count = data_v.shape[0]
    last = blocks - 1
    lower, upper, middle = pl.ds(tile_rows, s), pl.ds(0, s), pl.ds(s, tile_rows - s)

    pairs = [
        (rows_hbm, rows_ref),
        (cols_hbm, cols_ref),
        (probe_hbm, probe_v),
    ]
    for block in range(blocks):
        pairs.append((copy_hbm.at[:, :, pl.ds(block * s, s)], copy_v.at[:, block]))
    needed = len(pairs)
    for part in range(count // BATCH):
        span = pl.ds(part * BATCH, BATCH)
        pairs.append((data_hbm.at[span], data_v.at[span]))
    early = len(pairs) - count // BATCH + 1
    for block in range(last):
        pairs.append((cons_hbm.at[:, :, pl.ds(block * s, s)], cons_v.at[:, block, pl.ds(0, tile_rows)]))
    pairs.append((dual_hbm, dual_v))
    loads = [
        pltpu.make_async_copy(source, target, load_sems.at[index])
        for index, (source, target) in enumerate(pairs)
    ]
    for load in loads[:early] + loads[-1 - last : -1]:
        load.start()

    def row_peer(index):
        return (index, b)

    def col_peer(index):
        return (a, index)

    barrier = pltpu.get_barrier_semaphore()
    for peer, mine, size in ((row_peer, a, n_row), (col_peer, b, n_col)):

        def greet(hop, carry):
            pl.semaphore_signal(
                barrier, inc=1, device_id=peer(lax.rem(mine + hop, size)), device_id_type=MESH
            )
            return carry

        lax.fori_loop(1, size, greet, 0)

    fill_tables(tables_v)
    terms_v[...] = jnp.zeros_like(terms_v)
    grad_v[...] = jnp.zeros_like(grad_v)
    probe_grad_v[...] = jnp.zeros_like(probe_grad_v)

    def remote(source, target, send_sem, recv_sem, device):
        return pltpu.make_async_remote_copy(
            src_ref=source, dst_ref=target, send_sem=send_sem, recv_sem=recv_sem,
            device_id=device, device_id_type=MESH,
        )

    class Spread:
        def __init__(self, phase, peer, mine, size, source_of, slots):
            def move(hop, other):
                return remote(
                    source_of(other), slots.at[mine], sum_send.at[phase, hop], sum_recv.at[phase, hop], peer(other)
                )

            def start(hop, carry):
                move(hop, lax.rem(mine + hop, size)).start()
                return carry

            def arrive(hop, carry):
                other = lax.rem(mine + size - hop, size)
                remote(
                    source_of(other), slots.at[other], sum_send.at[phase, hop], sum_recv.at[phase, hop], peer(other)
                ).wait_recv()
                return carry

            def leave(hop, carry):
                move(hop, lax.rem(mine + hop, size)).wait_send()
                return carry

            lax.fori_loop(1, size, start, 0)
            self.arrived = lambda: lax.fori_loop(1, size, arrive, 0)
            self.left = lambda: lax.fori_loop(1, size, leave, 0)

    class Halo:
        def __init__(self, index, source, target, sends, device, receives):
            move = remote(source, target, halo_send.at[index], halo_recv.at[index], device)
            self.move, self.sends, self.receives = move, sends, receives

        def start(self):
            pl.when(self.sends)(lambda: self.move.start())

        def arrived(self):
            pl.when(self.receives)(lambda: self.move.wait_recv())

        def left(self):
            pl.when(self.sends)(lambda: self.move.wait_send())

    up, down, left, right = (a - 1, b), (a + 1, b), (a, b - 1), (a, b + 1)
    is_up, is_down, is_left, is_right = a > 0, a < n_row - 1, b > 0, b < n_col - 1
    has_up, has_down = is_up.astype(F32), is_down.astype(F32)
    has_left, has_right = is_left.astype(F32), is_right.astype(F32)
    own_rows = pl.ds(0, tile_rows)
    cons_left = Halo(
        0, cons_v.at[:, 0, own_rows], cons_v.at[:, last, own_rows], is_left, left, is_right
    )
    inner = pl.ds(0, last)
    cons_up = Halo(1, cons_v.at[:, inner, upper], cons_v.at[:, inner, lower], is_up, up, is_down)
    cons_corner = Halo(2, cons_v.at[:, last, upper], cons_v.at[:, last, lower], is_up, up, is_down)

    lane = lax.broadcasted_iota(jnp.int32, (s, s), 1)

    def place(member):
        top = rows_ref[member] & (tile_rows - 1)
        left_col = cols_ref[member] & (tile_cols - 1)
        return top, left_col // s, left_col % s

    def collect(batch):
        spots = [place(batch * BATCH + member) for member in range(BATCH)]
        for first in range(0, ext_rows, s):
            span = pl.ds(first, s)
            rows = [jnp.clip(first - top, -s, s) + s for top, _, _ in spots]
            for part in range(2):
                for block in range(blocks):
                    total = grad_v[part, block, span, :]
                    for member in range(BATCH):
                        _, home, _ = spots[member]
                        kind = jnp.clip(block - home, 0, 1)
                        row = jnp.where(kind == block - home, rows[member], 0)
                        total = total + terms_v[kind, member, part, pl.ds(row, s), :]
                    grad_v[part, block, span, :] = total

    for load in loads[:needed]:
        load.wait()
    for load in loads[early : early + count // BATCH - 1] + loads[-1:]:
        load.start()

    def work(index, carry):
        loads_data(index).wait()

        pl.when(index > 0)(lambda: collect(index - 1))

        @pl.when(index == 1)
        def _():
            pl.semaphore_wait(barrier, n_row + n_col - 2)
            for load in loads[-1 - last : -1]:
                load.wait()
            cons_up.start()
            cons_left.start()

        forward = (tables_v[0], tables_v[1])
        backward = (tables_v[2], tables_v[3])
        probe_re, probe_im = probe_v[0], probe_v[1]
        spots, fields = [], []
        for member in range(BATCH):
            top, block, shift = place(index * BATCH + member)
            spots.append(shift)
            field = []
            for part in range(2):
                near = copy_v[part, block, pl.ds(top, s), :]
                far = copy_v[part, block + 1, pl.ds(top, s), :]
                field.append(pltpu.roll(jnp.where(lane >= shift, near, far), (s - shift) % s, 1))
            fields.append(field)
        sum_re = jnp.zeros((s, s), F32)
        sum_im = jnp.zeros((s, s), F32)
        waves = []
        for re, im in fields:
            waves.append(
                jnp.concatenate([probe_re * re - probe_im * im, probe_re * im + probe_im * re], 1)
            )
        rows_done = times_right(jnp.concatenate(waves, 0), *forward)
        misfits = []
        for first in range(0, BATCH, 2):
            spectrum = times_left(*backward, swapped(rows_done[first * s : (first + 2) * s]))
            spec_re, spec_im = spectrum[:s], spectrum[s:]
            data = jnp.concatenate(
                [data_v[index * BATCH + first], data_v[index * BATCH + first + 1]], 1
            )
            residue = spec_re * spec_re + spec_im * spec_im - data
            weighted = jnp.concatenate([residue * spec_re, residue * spec_im], 0)
            misfits.append(swapped(times_left(*forward, weighted)))
        misfit = times_right(jnp.concatenate(misfits, 0), *backward)
        for member in range(BATCH):
            mis_re = misfit[member * s : (member + 1) * s, :s]
            mis_im = misfit[member * s : (member + 1) * s, s:]
            re, im = fields[member]
            sum_re += re * mis_re + im * mis_im
            sum_im += re * mis_im - im * mis_re
            shift = spots[member]
            terms = (probe_re * mis_re + probe_im * mis_im, probe_re * mis_im - probe_im * mis_re)
            for part in range(2):
                term = pltpu.roll(terms[part], shift, 1)
                terms_v[0, member, part, pl.ds(s, s), :] = jnp.where(lane >= shift, term, 0.0)
                terms_v[1, member, part, pl.ds(s, s), :] = jnp.where(lane >= shift, 0.0, term)
        probe_grad_v[0] += sum_re
        probe_grad_v[1] += sum_im
        return carry

    def loads_data(index):
        span = pl.ds(index * BATCH, BATCH)
        return pltpu.make_async_copy(data_hbm.at[span], data_v.at[span], load_sems.at[needed + index])

    lax.fori_loop(0, count // BATCH, work, 0)
    collect(count // BATCH - 1)

    def squares(index, total):
        for part in range(2):
            for block in range(blocks):
                value = grad_v[part, block, pl.ds(pl.multiple_of(index * 8, 8), 8), :]
                total = total + value * value
        return total

    norm = lax.fori_loop(0, ext_rows // 8, squares, jnp.zeros((8, s), F32))

    piece = col_out.shape[1] - 8
    for index in range(n_col):
        first = index * piece
        col_out[index, :piece] = probe_grad_v[first // s, pl.ds(first % s, piece), :]
        col_out[index, piece:] = norm
    first_sum = Spread(0, col_peer, b, n_col, lambda other: col_out.at[other], col_in)
    col_in[b] = col_out[b]

    loads[-1].wait()

    first_sum.arrived()

    def total_of(slots, size):
        total = slots[0]
        for index in range(1, size):
            total = total + slots[index]
        return total

    row_out[...] = total_of(col_in, n_col)
    second_sum = Spread(1, row_peer, a, n_row, lambda other: row_out, row_in)
    row_in[a] = row_out[...]
    second_sum.arrived()
    whole = total_of(row_in, n_row)
    total_squares = jnp.sum(whole[piece:], keepdims=True)
    scale = object_step / jnp.sqrt(total_squares / (n_row * n_col * ext_rows * ext_cols) + epsilon)
    keep = 1.0 - object_step * penalty
    pull = object_step * penalty

    def fill(first, size, block):
        columns = pl.ds(block * s, s)
        span = pl.ds(first, size)
        for part in range(2):
            old, dual = copy_v[part, block, span], dual_v[part, span, columns]
            w_v[part, block, span, :] = keep * (old + dual) - scale * grad_v[part, block, span, :]

    order = [(part, block) for block in [0, last] + list(range(1, last)) for part in range(2)]
    rows_up, rows_down = {}, {}
    for index, (part, block) in enumerate(order):
        rows_up[part, block] = Halo(
            3 + index, w_v.at[part, block, upper], from_down.at[part, block], is_up, up, is_down
        )
        rows_down[part, block] = Halo(
            3 + len(order) + index, w_v.at[part, block, lower], from_up.at[part, block], is_down, down, is_up
        )
    used = 3 + 2 * len(order)
    half, edge = n_col // 2, n_col - 1
    relays = n_col > 2
    via_last, via_first = (b == half) & relays, (b == half - 1) & relays
    size = tile_rows - s
    pieces = [
        (1, pl.ds(s, size), True),
        (0, pl.ds(s, size // 2), True),
        (0, pl.ds(s + size // 2, size // 2), False),
    ]
    to_left, to_right, onward_left, onward_right = [], [], [], []
    for part, span, relayed in pieces:
        target_left, target_right = b - 1, b + 1
        if relayed:
            target_left = jnp.where(via_last, edge, b - 1)
            target_right = jnp.where(via_first, 0, b + 1)
            onward_left.append(
                Halo(used, from_right.at[part, span], from_right.at[part, span], b == edge, (a, half - 1), False)
            )
            onward_right.append(
                Halo(used + 1, from_left.at[part, span], from_left.at[part, span], b == 0, (a, half), False)
            )
        to_left.append(
            Halo(used, w_v.at[part, 0, span], from_right.at[part, span], is_left, (a, target_left), is_right)
        )
        to_right.append(
            Halo(used + 1, w_v.at[part, last, span], from_left.at[part, span], is_right, (a, target_right), is_left)
        )
        used += 2

    def relay(index):
        if relays:
            for flag, move, onward in (
                (b == edge, to_left[index], onward_left[index]),
                (b == 0, to_right[index], onward_right[index]),
            ):

                @pl.when(flag)
                def _():
                    move.move.wait_recv()
                    onward.move.start()

    corners = {}
    for part in range(2):
        for block, target, sends, device, receives in (
            (0, from_right, is_left, left, is_right),
            (last, from_left, is_right, right, is_left),
        ):
            for source, span in ((from_up, upper), (from_down, lower)):
                corners[part, block, span is upper] = Halo(
                    used, source.at[part, block], target.at[part, span], sends, device, receives
                )
                used += 1
    col_all[b] = whole[:piece]
    third_sum = Spread(2, col_peer, b, n_col, lambda other: col_all.at[b], col_all)
    for block in (0, last):
        fill(0, s, block)
        fill(tile_rows, s, block)
        for part in range(2):
            rows_up[part, block].start()
            rows_down[part, block].start()
    fill(s, tile_rows - s, 0)
    for move in to_left:
        move.start()
    fill(s, tile_rows - s, last)
    for move in to_right:
        move.start()
    for block in range(1, last):
        fill(0, s, block)
        fill(tile_rows, s, block)
        for part in range(2):
            rows_up[part, block].start()
            rows_down[part, block].start()
    for block in range(1, last):
        fill(s, tile_rows - s, block)

    def neighbour(present, value):
        return jnp.where(present, value, 0.0)

    def join(part, block):
        rows_up[part, block].arrived()
        rows_down[part, block].arrived()
        from_up[part, block] = w_v[part, block, upper] + neighbour(is_up, from_up[part, block])
        from_down[part, block] = w_v[part, block, lower] + neighbour(is_down, from_down[part, block])

    relay(0)
    for block in (0, last):
        for part in range(2):
            join(part, block)
            corners[part, block, True].start()
            corners[part, block, False].start()

    relay(1)

    cons_left.arrived()
    pl.when(jnp.logical_not(is_right))(
        lambda: cons_v.__setitem__((slice(None), last, own_rows), jnp.zeros((2, tile_rows, s), F32))
    )
    cons_corner.start()
    pl.when(jnp.logical_not(is_down))(
        lambda: cons_v.__setitem__((slice(None), slice(None), lower), jnp.zeros((2, blocks, s, s), F32))
    )
    cons_up.arrived()

    def renew(span, block):
        columns = pl.ds(block * s, s)
        for part in range(2):
            new_copy_ref[part, span, columns] = (
                w_v[part, block, span] - dual_v[part, span, columns] + pull * cons_v[part, block, span]
            )

    for block in range(blocks):
        renew(own_rows, block)
        if block < last:
            renew(lower, block)
    for part in range(2):
        for block in range(1, last):
            columns = pl.ds(block * s, s)
            new_cons_ref[part, middle, columns] = w_v[part, block, middle] + pull * cons_v[part, block, middle]
            new_dual_ref[part, middle, columns] = jnp.zeros((tile_rows - s, s), F32)

    def finish(span, block, total, cover_rows, inside_rows):
        columns = pl.ds(block * s, s)
        for part in range(2):
            summed = total(part)
            cover = cover_rows
            inside = inside_rows
            if block == 0:
                summed = summed + neighbour(is_left, from_left[part, span])
                cover = cover * (1.0 + has_left)
            if block == last:
                summed = summed + neighbour(is_right, from_right[part, span])
                cover = cover * (1.0 + has_right)
                inside = inside * has_right
            mean = summed * (1.0 / cover)
            new_dual_ref[part, span, columns] = w_v[part, block, span] - inside * mean
            if block < last and span is not lower:
                new_cons_ref[part, span, columns] = mean + pull * cons_v[part, block, span]

    one = jnp.float32(1.0)

    def top_and_bottom(block):
        finish(upper, block, lambda part: from_up[part, block], 1.0 + has_up, one)
        finish(lower, block, lambda part: from_down[part, block], 1.0 + has_down, has_down)

    for block in range(1, last):
        for part in range(2):
            join(part, block)
        top_and_bottom(block)
    for move in to_left + to_right:
        move.arrived()
    for block in (0, last):
        finish(middle, block, lambda part: w_v[part, block, middle], one, one)

    third_sum.arrived()
    power = jnp.zeros((piece, s), F32)
    for index in range(n_col):
        power = power + col_all[index] * col_all[index]
    rate = probe_step / jnp.sqrt(jnp.sum(power, keepdims=True) / (s * s) + epsilon)
    for index in range(n_col):
        first = index * piece
        half, span = first // s, pl.ds(first % s, piece)
        new_probe_ref[half, span, :] = probe_v[half, span, :] - rate * col_all[index]

    cons_corner.arrived()
    renew(lower, last)
    for corner in corners.values():
        corner.arrived()
    for block in (0, last):
        top_and_bottom(block)

    halos = [cons_left, cons_up, cons_corner] + to_left + to_right + (onward_left + onward_right if relays else [])
    for group in (rows_up, rows_down, corners):
        halos += list(group.values())
    for move in halos + [first_sum, second_sum, third_sum]:
        move.left()


def step(n_row, n_col, pos_rows, pos_cols, local_copy, dual, consensus, probe, intensity):
    s = SIDE
    count = intensity.shape[0]
    ext_rows, ext_cols = local_copy.shape[1:]
    blocks = ext_cols // s
    piece = 2 * s // n_col
    vmem, hbm = pl.BlockSpec(memory_space=pltpu.VMEM), pl.BlockSpec(memory_space=pltpu.HBM)
    halos = 3 + 4 * blocks + 6 + 8
    return pl.pallas_call(
        functools.partial(step_body, n_row, n_col),
        in_specs=[hbm] * 7,
        out_specs=[vmem] * 4,
        out_shape=[
            jax.ShapeDtypeStruct(local_copy.shape, F32),
            jax.ShapeDtypeStruct(consensus.shape, F32),
            jax.ShapeDtypeStruct(local_copy.shape, F32),
            jax.ShapeDtypeStruct(probe.shape, F32),
        ],
        scratch_shapes=[
            pltpu.SMEM(pos_rows.shape, jnp.int32),
            pltpu.SMEM(pos_cols.shape, jnp.int32),
            pltpu.VMEM((2, blocks, ext_rows, s), F32),
            pltpu.VMEM(dual.shape, F32),
            pltpu.VMEM((2, blocks, ext_rows, s), F32),
            pltpu.VMEM(probe.shape, F32),
            pltpu.VMEM(intensity.shape, F32),
            pltpu.VMEM((4, 2 * s, 2 * s), BF16),
            pltpu.VMEM((2, BATCH, 2, 3 * s, s), F32),
            pltpu.VMEM((2, blocks, ext_rows, s), F32),
            pltpu.VMEM((2, s, s), F32),
            pltpu.VMEM((2, blocks, ext_rows, s), F32),
            pltpu.VMEM((2, blocks, s, s), F32),
            pltpu.VMEM((2, blocks, s, s), F32),
            pltpu.VMEM((2, ext_rows, s), F32),
            pltpu.VMEM((2, ext_rows, s), F32),
            pltpu.VMEM((n_col, piece + 8, s), F32),
            pltpu.VMEM((n_col, piece + 8, s), F32),
            pltpu.VMEM((piece + 8, s), F32),
            pltpu.VMEM((n_row, piece + 8, s), F32),
            pltpu.VMEM((n_col, piece, s), F32),
            pltpu.SemaphoreType.DMA((3 + blocks + count // BATCH + blocks,)),
            pltpu.SemaphoreType.DMA((halos,)),
            pltpu.SemaphoreType.DMA((halos,)),
            pltpu.SemaphoreType.DMA((3, max(n_row, n_col))),
            pltpu.SemaphoreType.DMA((3, max(n_row, n_col))),
        ],
        compiler_params=pltpu.CompilerParams(
            collective_id=0, has_side_effects=True, vmem_limit_bytes=46 * 2**20
        ),
        cost_estimate=pl.CostEstimate(
            flops=count * 4 * 3 * 2 * s * 256 * 256, bytes_accessed=16 * 2**20, transcendentals=0
        ),
    )(pos_rows, pos_cols, local_copy, dual, consensus, probe, intensity)


def store_body(*refs):
    count = len(refs) // 2
    sources, targets, sems = refs[:count], refs[count : 2 * count], refs[2 * count]
    moves = [
        pltpu.make_async_copy(source.at[part], target.at[part], sems.at[index, part])
        for index, (source, target) in enumerate(zip(sources, targets))
        for part in range(2)
    ]
    for move in moves:
        move.start()
    for move in moves:
        move.wait()


def store(*arrays):
    return pl.pallas_call(
        store_body,
        in_specs=[pl.BlockSpec(memory_space=pltpu.VMEM)] * len(arrays),
        out_specs=[pl.BlockSpec(memory_space=pl.ANY)] * len(arrays),
        out_shape=[jax.ShapeDtypeStruct(array.shape, F32) for array in arrays],
        scratch_shapes=[pltpu.SemaphoreType.DMA((len(arrays), 2))],
        compiler_params=pltpu.CompilerParams(vmem_limit_bytes=16 * 2**20),
    )(*arrays)


def per_device(n_row, n_col, local_copy, dual, consensus, probe, intensity, pos_rows, pos_cols):
    new_copy, new_consensus, new_dual, new_probe = step(
        n_row, n_col, pos_rows, pos_cols, local_copy, dual, consensus, probe, intensity
    )
    return tuple(store(new_copy, new_consensus, new_dual, new_probe))


def solution(mesh):
    field = P(None, "row", "col")
    both = ("row", "col")
    return jax.shard_map(
        functools.partial(per_device, mesh.shape["row"], mesh.shape["col"]),
        mesh=mesh,
        in_specs=(field, field, field, P(), P(both, None, None), P(both), P(both)),
        out_specs=(field, field, field, P()),
        check_vma=False,
    )
```
